512 devices in a mesh: ctx: 64 (over z, x, core), tp: 8 (over y).
Axes of the slice: x: 4, y: 8, z: 8, core: 2. Of those that a mesh axis runs over, the one named last changes fastest.
Arguments:
- streams: bfloat16 [3, 24576, 8192], P(None, 'ctx', 'tp'), may hold values from -6 to 6
- filters: float32 [3, 7, 8192], P(None, None, 'tp'), may hold values from -3 to 3
- out_weight: bfloat16 [8192, 4096], P('tp', 'ctx'), may hold values from -0.09375 to 0.09375
- grad_out: bfloat16 [24576, 4096], P('ctx', 'tp'), may hold values from -6 to 6
- counts: int32 [64], P('ctx'), may hold values from 192 to 384, as said below
- starts: int32 [64], P('ctx'), may hold values from 0 to 18240, as said below
Outputs:
- grad_payload: bfloat16 [3, 24576, 8192], P(None, 'ctx', 'tp')
- grad_scales: float32 [3, 256, 8192], P(None, 'ctx', 'tp')
- filter_grad: float32 [3, 7, 8192], P(None, None, 'tp')
The draws below stay inside these ranges and needn't reach their ends.
Inputs may be any that keep to these rules, and one draw needn't show every extreme that they name: `counts`: each device holds 192 to 384 tokens; they sum to 18432; some device holds exactly 384 and some exactly 192. starts[i] is the sum of counts of devices before i.
All inputs are finite; a program needn't handle non-finite values. Where the reference program divides by a largest or mean magnitude, that divisor is 1e-20 or more.
Results may differ from the reference program's by a relative error of at most 0.015.
Values may be sent and summed in bfloat16 or wider, within the bound.
A program may use at most 64 MiB of HBM per device.

```python
import jax
import jax.numpy as jnp

D = 8192
OUTW = 4096
KS = 7
TILE = 128
CAP = 384
SLOTS = 4
ROWS = 24576
TOTAL = 18432
N_CTX = 64


def split_tokens(key):
    pairs = N_CTX // 2
    lower = CAP // 2
    extra = jax.random.randint(jax.random.fold_in(key, 11), (pairs,), 0, lower + 1)
    chosen = jax.random.randint(jax.random.fold_in(key, 12), (), 0, pairs)
    extra = jnp.where(jnp.arange(pairs) == chosen, lower, extra)
    values = jnp.concatenate([lower + extra, lower + (lower - extra)])
    order = jax.random.permutation(jax.random.fold_in(key, 13), N_CTX)
    sizes_here = values[order].astype(jnp.int32)
    firsts = (jnp.cumsum(sizes_here) - sizes_here).astype(jnp.int32)
    return (sizes_here, firsts)


def draw_counts(key, part):
    return split_tokens(key)[0]


def draw_starts(key, part):
    return split_tokens(key)[1]


def level_of(rng, dims, pieces, smallest, largest):
    loudness = 1.0
    for position, blocks in pieces:
        draws = jax.random.uniform(jax.random.fold_in(jax.random.fold_in(rng, 6), position), (blocks,), jnp.float32, smallest / len(pieces), largest / len(pieces))
        loudness = loudness * jnp.repeat(jnp.exp(draws), dims[position] // blocks).reshape((-1,) + (1,) * (len(dims) - 1 - position))
    return loudness


def bell_draw(stream_key, extent, deviation, most, pieces=(), kind=jnp.bfloat16):
    drawn = deviation * jax.random.normal(stream_key, extent, jnp.float32)
    if pieces:
        drawn = drawn * level_of(stream_key, extent, pieces, -0.22, 0.18)
    return jnp.clip(drawn, -most, most).astype(kind)


def setup_inputs(seed: int = 0) -> dict:
    keys = jax.random.split(jax.random.key(seed), 7)
    return {
        "streams": bell_draw(keys[0], (3, ROWS, D), 1.0, 6.0, ((1, 64), (2, 8))),
        "filters": bell_draw(keys[1], (3, KS, D), 0.5, 3.0, ((2, 8),), jnp.float32),
        "out_weight": bell_draw(keys[2], (D, OUTW), OUTW ** -0.5, 0.09375, ((0, 8), (1, 64))),
        "grad_out": bell_draw(keys[3], (ROWS, OUTW), 1.0, 6.0, ((0, 64), (1, 8))),
        "counts": draw_counts(jax.random.fold_in(keys[6], 71), 0),
        "starts": draw_starts(jax.random.fold_in(keys[6], 71), 0),
    }


def reference(streams, filters, out_weight, grad_out, counts, starts):
    rowid = jnp.arange(CAP, dtype=jnp.int32)
    usable = (rowid[None, :] < counts[:, None]).reshape(-1)
    places = (starts[:, None] + rowid[None, :]).reshape(-1)
    target = jnp.where(usable, places, TOTAL).astype(jnp.int32)
    source = jnp.clip(target, 0, TOTAL - 1).astype(jnp.int32)

    def compact(values):
        return jnp.zeros((TOTAL,) + values.shape[1:], values.dtype).at[target].set(values, mode="drop")

    grad_gate = jnp.dot(grad_out, out_weight.T, preferred_element_type=jnp.float32).astype(jnp.bfloat16)
    gate_rows = compact(grad_gate).astype(jnp.float32)
    padded_u = []
    filtered = []
    for s in range(3):
        padded = jnp.pad(compact(streams[s]).astype(jnp.float32), ((KS - 1, 0), (0, 0)))
        padded_u.append(padded)
        acc = jnp.zeros((TOTAL, D), jnp.float32)
        for j in range(KS):
            acc = acc + filters[s, j][None, :] * padded[KS - 1 - j:KS - 1 - j + TOTAL]
        filtered.append(acc)
    grad_conv = [
        (gate_rows * filtered[1] * filtered[2]).astype(jnp.bfloat16),
        (gate_rows * filtered[0] * filtered[2]).astype(jnp.bfloat16),
        (gate_rows * filtered[0] * filtered[1]).astype(jnp.bfloat16),
    ]
    payloads = []
    slot_scales = []
    taps_grad = []
    tile_first = starts // TILE
    tile_last = (starts + counts - 1) // TILE
    tile_ids = tile_first[:, None] + jnp.arange(SLOTS, dtype=jnp.int32)[None, :]
    tile_used = tile_ids <= tile_last[:, None]
    for s in range(3):
        grad_float = grad_conv[s].astype(jnp.float32)
        after = jnp.pad(grad_float, ((0, KS - 1), (0, 0)))
        grad_input = jnp.zeros((TOTAL, D), jnp.float32)
        rows_grad = []
        for j in range(KS):
            grad_input = grad_input + filters[s, j][None, :] * after[j:j + TOTAL]
            rows_grad.append(jnp.sum(grad_float * padded_u[s][KS - 1 - j:KS - 1 - j + TOTAL], axis=0))
        taps_grad.append(jnp.stack(rows_grad, axis=0))
        scale = jnp.max(jnp.abs(grad_input).reshape(TOTAL // TILE, TILE, D), axis=1) + 1e-6
        payload = (grad_input / jnp.repeat(scale, TILE, axis=0)).astype(jnp.bfloat16)
        payload = jnp.where(usable[:, None], payload[source], jnp.zeros((), jnp.bfloat16))
        payloads.append(payload)
        picked = scale[jnp.clip(tile_ids, 0, TOTAL // TILE - 1).astype(jnp.int32)]
        picked = jnp.where(tile_used[:, :, None], picked, 0.0)
        slot_scales.append(picked.reshape(N_CTX * SLOTS, D))
    return jnp.stack(payloads, axis=0), jnp.stack(slot_scales, axis=0), jnp.stack(taps_grad, axis=0)
```

```python
import functools

import jax
import jax.numpy as jnp
from jax import lax
from jax.experimental import pallas as pl
from jax.experimental.pallas import tpu as pltpu
from jax.sharding import PartitionSpec as P

MESH = pl.DeviceIdType.MESH
TILE = 128
LANES = 128
NZ, NX, NC, NY = 8, 4, 2, 8
NG = NX * NC
CH = 64
SLOTS = 4


def kernel(
    streams_ref, filters_ref, weight_ref, grad_ref, counts_ref, starts_ref,
    pay_ref, scales_ref, fgrad_ref,
    sv, u32, prod, wt, gg, dy32, dc32, du32, tail, halo, head, heads_in, zbuf,
    msc, isc, tmx, max_prev, max_next, fsc, p1, p2, tot,
    send, recv, local,
):
    rows = grad_ref.shape[0]
    width = grad_ref.shape[1]
    taps = filters_ref.shape[1]
    groups = weight_ref.shape[0] // LANES
    i = lax.axis_index("ctx")
    y = lax.axis_index("tp")
    z = i // NG
    q = i % NG
    x = q // NC
    core = q % NC
    n_ctx = NZ * NG

    count = counts_ref[0]
    first = starts_ref[0]
    offset = first % TILE
    last_slot = jnp.clip((offset + count - 1) // TILE, 0, SLOTS - 1)

    def at(zz, xx, cc):
        return ((zz + NZ) % NZ) * NG + ((xx + NX) % NX) * NC + cc

    copies = []

    def push(src, dst, ctx, tp):
        k = len(copies)
        c = pltpu.make_async_remote_copy(
            src_ref=src, dst_ref=dst, send_sem=send.at[k], recv_sem=recv.at[k],
            device_id=(ctx, tp), device_id_type=MESH,
        )
        c.start()
        copies.append(c)
        return c

    up, down = (i + 1) % n_ctx, (i + n_ctx - 1) % n_ctx
    yr, yl = (y + 1) % NY, (y + NY - 1) % NY
    zr, zl = at(z + 1, x, core), at(z - 1, x, core)
    xr, xl = at(z, x + 1, core), at(z, x - 1, core)
    mate = at(z, x, 1 - core)

    get_streams = pltpu.make_async_copy(streams_ref, sv, local.at[0])
    get_streams.start()
    own_cols = pl.ds(pl.multiple_of(y * width, width), width)
    get_grad = pltpu.make_async_copy(grad_ref, gg.at[:, own_cols], local.at[1])
    get_grad.start()

    barrier = pltpu.get_barrier_semaphore()
    peers = [(i, yr), (i, yl), (up, y), (down, y)]
    peers += [(z * NG + (q + d) % NG, y) for d in range(1, NG)]
    peers += [(((z + d) % NZ) * NG + q, y) for d in range(1, NZ)]
    for peer in peers:
        pl.semaphore_signal(barrier, inc=1, device_id=peer, device_id_type=MESH)
    wt[z, x, core] = weight_ref[...].T
    pl.semaphore_wait(barrier, len(peers))

    half = rows // 2

    def gblock(c, t):
        t = (t + NY) % NY
        return gg.at[pl.ds(c * half, half), pl.ds(pl.multiple_of(t * width, width), width)]

    def gstep(c, d):
        out = []
        if d < 4 or c == 0:
            src = gblock(c, y - d + 1) if d > 1 else grad_ref.at[pl.ds(c * half, half)]
            out.append(push(src, gblock(c, y - d + 1), i, yr))
        if d < 4 or c == 1:
            src = gblock(c, y + d - 1) if d > 1 else grad_ref.at[pl.ds(c * half, half)]
            out.append(push(src, gblock(c, y + d - 1), i, yl))
        return out

    def arrived(cs):
        for c in cs:
            c.wait_recv()

    def ablock(zz, lo=0, n=NX):
        return wt.at[(zz + NZ) % NZ, pl.ds(lo, n), core, pl.ds(0, 32), :]

    def bpiece(zz, lo=32, n=32):
        return wt.at[(zz + NZ) % NZ, x, core, pl.ds(lo, n), :]

    def bblock(xx, lo=0, n=NZ):
        return wt.at[pl.ds(lo, n), (xx + NX) % NX, core, pl.ds(32, 32), :]

    def bstep(d):
        n = 32 if d < 4 else 16
        lo = 32 if d < 4 else 48
        return [
            push(bpiece(z - d + 1, 32, n), bpiece(z - d + 1, 32, n), zr, y),
            push(bpiece(z + d - 1, lo, n), bpiece(z + d - 1, lo, n), zl, y),
        ]

    def astep(d):
        n = NX if d < 4 else NX // 2
        lo = 0 if d < 4 else NX // 2
        return [
            push(ablock(z - d + 1, 0, n), ablock(z - d + 1, 0, n), zr, y),
            push(ablock(z + d - 1, lo, n), ablock(z + d - 1, lo, n), zl, y),
        ]

    g0 = gstep(0, 1)
    own = wt.at[z, x, core, pl.ds(0, 32), :]
    a1 = [push(own, own, at(z, x + d, core), y) for d in range(1, NX)]
    b1 = bstep(1)
    g1 = gstep(1, 1)

    get_streams.wait()

    def widen(cg, _):
        lanes = pl.ds(pl.multiple_of(cg * LANES, LANES), LANES)
        for s in range(3):
            u32[s, cg, 8 : 8 + rows, :] = sv[s, :, lanes].astype(jnp.float32)
            tail[s, cg] = u32[s, cg, pl.ds(jnp.clip(count, 8, rows), 8), :]
        return 0

    lax.fori_loop(0, groups, widen, 0)
    tails = push(tail, halo, up, y)

    arrived(b1)
    b2 = bstep(2)
    arrived(a1)
    mates = [push(ablock(z), ablock(z), mate, y)]
    a2 = astep(1)
    arrived(b2)
    b3 = bstep(3)
    arrived(g0)
    g0 = gstep(0, 2)
    arrived(b3)
    b4 = bstep(4)
    arrived(b4)
    bx = [push(bblock(x), bblock(x), xr, y), push(bblock(x), bblock(x), xl, y)]
    mates.append(push(bblock(x), bblock(x), mate, y))

    tails.wait_recv()

    def forward(cg, _):
        lanes = pl.ds(pl.multiple_of(cg * LANES, LANES), LANES)
        coef = []
        for s in range(3):
            u32[s, cg, 0:8, :] = jnp.where(i > 0, halo[s, cg], 0.0)
            du32[s, cg, 0:TILE, :] = jnp.zeros((TILE, LANES), jnp.float32)
            du32[s, cg, TILE + rows :, :] = jnp.zeros((TILE, LANES), jnp.float32)
            dc32[s, cg, rows:, :] = jnp.zeros((8, LANES), jnp.float32)
            zbuf[s, cg] = jnp.zeros((24, LANES), jnp.float32)
            coef.append([filters_ref[s, pl.ds(j, 1), lanes] for j in range(taps)])

        def chunk(r, _):
            r0 = pl.multiple_of(r * CH, CH)
            c = []
            for s in range(3):
                acc = coef[s][0] * u32[s, cg, pl.ds(8 + r0, CH), :]
                for j in range(1, taps):
                    acc = acc + coef[s][j] * u32[s, cg, pl.ds(8 + r0 - j, CH), :]
                c.append(acc)
            prod[0, cg, pl.ds(r0, CH), :] = c[1] * c[2]
            prod[1, cg, pl.ds(r0, CH), :] = c[0] * c[2]
            prod[2, cg, pl.ds(r0, CH), :] = c[0] * c[1]
            return 0

        lax.fori_loop(0, rows // CH, chunk, 0)
        return 0

    lax.fori_loop(0, groups, forward, 0)

    arrived(g1)
    g1 = gstep(1, 2)
    for d in range(1, 4):
        arrived(a2)
        if d == 3:
            arrived(bx)
            mates.append(push(bblock(x - 1), bblock(x - 1), mate, y))
            mates.append(push(bblock(x + 1), bblock(x + 1), mate, y))
            bx = [
                push(bblock(x - 1, 0, 4), bblock(x - 1, 0, 4), xr, y),
                push(bblock(x + 1, 4, 4), bblock(x + 1, 4, 4), xl, y),
            ]
        a2 = astep(d + 1)
        mates.append(push(ablock(z - d), ablock(z - d), mate, y))
        mates.append(push(ablock(z + d), ablock(z + d), mate, y))
        if d < 3:
            arrived(g0)
            g0 = gstep(0, d + 2)
            arrived(g1)
            g1 = gstep(1, d + 2)
    arrived(a2)
    mates.append(push(ablock(z + 4), ablock(z + 4), mate, y))
    arrived(bx)
    mates.append(push(bblock(x + 2), bblock(x + 2), mate, y))
    get_grad.wait()
    arrived(mates)
    arrived(g0)
    arrived(g1)

    def project(n, _):
        cols = pl.ds(pl.multiple_of(n * 256, 256), 256)
        w = wt[:, :, :, :, cols].reshape(NZ * NG * 64, 256)
        dy = jnp.dot(gg[...], w, preferred_element_type=jnp.float32)
        dy = dy.astype(jnp.bfloat16).astype(jnp.float32)
        dy32[2 * n] = dy[:, :LANES]
        dy32[2 * n + 1] = dy[:, LANES:]
        return 0

    lax.fori_loop(0, groups // 2, project, 0)

    def gate(cg, _):
        def chunk(r, _):
            r0 = pl.multiple_of(r * CH, CH)
            live = lax.broadcasted_iota(jnp.int32, (CH, LANES), 0) + r0 < count
            dy = dy32[cg, pl.ds(r0, CH), :]
            for s in range(3):
                dc = jnp.where(live, dy * prod[s, cg, pl.ds(r0, CH), :], 0.0)
                dc32[s, cg, pl.ds(r0, CH), :] = dc.astype(jnp.bfloat16).astype(jnp.float32)
            return 0

        lax.fori_loop(0, rows // CH, chunk, 0)
        for s in range(3):
            head[s, cg] = dc32[s, cg, 0:8, :]
        return 0

    lax.fori_loop(0, groups, gate, 0)
    heads = push(head, heads_in, down, y)

    def correlate(cg, _):
        for s in range(3):
            def chunk(r, acc):
                r0 = pl.multiple_of(r * CH, CH)
                dc = dc32[s, cg, pl.ds(r0, CH), :]
                out = []
                for j in range(taps):
                    term = dc * u32[s, cg, pl.ds(8 + r0 - j, CH), :]
                    out.append(acc[j] + term.reshape(CH // 8, 8, LANES).sum(0))
                return tuple(out)

            zero = jnp.zeros((8, LANES), jnp.float32)
            acc = lax.fori_loop(0, rows // CH, chunk, (zero,) * taps)
            fsc[cg, s] = zero
            for j in range(taps):
                fsc[cg, s, j : j + 1, :] = acc[j].sum(0, keepdims=True)
        return 0

    lax.fori_loop(0, groups, correlate, 0)
    f1 = []
    for d in range(1, NG):
        to = (q + d) % NG
        f1.append(push(fsc.at[to], p1.at[d], z * NG + to, y))

    heads.wait_recv()

    def backward(cg, _):
        lanes = pl.ds(pl.multiple_of(cg * LANES, LANES), LANES)
        for s in range(3):
            zbuf[s, cg, 8:16, :] = jnp.where(i < n_ctx - 1, heads_in[s, cg], 0.0)

        def insert(r, _):
            r0 = pl.multiple_of(r * 8, 8)
            at_row = jnp.clip(r0 - count, -8, 8) + 8
            for s in range(3):
                dc32[s, cg, pl.ds(r0, 8), :] += zbuf[s, cg, pl.ds(at_row, 8), :]
            return 0

        lax.fori_loop(rows // 16, rows // 8 + 1, insert, 0)
        coef = [[filters_ref[s, pl.ds(j, 1), lanes] for j in range(taps)] for s in range(3)]

        def chunk(r, _):
            r0 = pl.multiple_of(r * CH, CH)
            live = lax.broadcasted_iota(jnp.int32, (CH, LANES), 0) + r0 < count
            for s in range(3):
                acc = coef[s][0] * dc32[s, cg, pl.ds(r0, CH), :]
                for j in range(1, taps):
                    acc = acc + coef[s][j] * dc32[s, cg, pl.ds(r0 + j, CH), :]
                du32[s, cg, pl.ds(TILE + r0, CH), :] = jnp.where(live, acc, 0.0)
            return 0

        lax.fori_loop(0, rows // CH, chunk, 0)

        for s in range(3):
            for k in range(SLOTS):
                block = jnp.abs(du32[s, cg, pl.ds((k + 1) * TILE - offset, TILE), :])
                top = block.reshape(TILE // 8, 8, LANES).max(0).max(0, keepdims=True)
                msc[k, pl.ds(s * groups + cg, 1), :] = top
        return 0

    lax.fori_loop(0, groups, backward, 0)
    tmx[...] = msc[last_slot]
    to_next = push(tmx, max_prev, up, y)
    to_prev = push(msc.at[0], max_next, down, y)

    arrived(f1)
    part = fsc[q]
    for d in range(1, NG):
        part = part + p1[d]
    p2[z] = part
    f2 = []
    for d in range(1, NZ):
        f2.append(push(p2.at[z], p2.at[z], ((z + d) % NZ) * NG + q, y))

    to_next.wait_recv()
    to_prev.wait_recv()
    prev = jnp.where(offset != 0, max_prev[...], 0.0)
    follow = jnp.where((first + count) % TILE != 0, max_next[...], 0.0)
    for k in range(SLOTS):
        top = msc[k]
        if k == 0:
            top = jnp.maximum(top, prev)
        top = jnp.maximum(top, jnp.where(last_slot == k, follow, 0.0))
        scale = top + 1e-6
        isc[k] = 1.0 / scale
        scale = jnp.where(last_slot >= k, scale, 0.0)
        for s in range(3):
            for cg in range(groups):
                row = s * groups + cg
                scales_ref[s, k : k + 1, cg * LANES : (cg + 1) * LANES] = scale[row : row + 1]

    def finish(cg, _):
        lanes = pl.ds(pl.multiple_of(cg * LANES, LANES), LANES)
        inv = [[isc[k, pl.ds(s * groups + cg, 1), :] for k in range(SLOTS)] for s in range(3)]

        def chunk(r, _):
            r0 = pl.multiple_of(r * CH, CH)
            pos = lax.broadcasted_iota(jnp.int32, (CH, LANES), 0) + (r0 + offset)
            for s in range(3):
                scale = jnp.where(pos >= 3 * TILE, inv[s][3], inv[s][2])
                scale = jnp.where(pos >= 2 * TILE, scale, inv[s][1])
                scale = jnp.where(pos >= TILE, scale, inv[s][0])
                du = du32[s, cg, pl.ds(TILE + r0, CH), :]
                pay_ref[s, pl.ds(r0, CH), lanes] = (du * scale).astype(jnp.bfloat16)
            return 0

        lax.fori_loop(0, rows // CH, chunk, 0)
        return 0

    lax.fori_loop(0, groups // 2, finish, 0)

    arrived(f2)
    total = p2[0]
    for d in range(1, NZ):
        total = total + p2[d]
    tot[q] = total
    f3 = []
    for d in range(1, NG):
        f3.append(push(tot.at[q], tot.at[q], z * NG + (q + d) % NG, y))

    lax.fori_loop(groups // 2, groups, finish, 0)

    arrived(f3)
    for cg in range(groups):
        for s in range(3):
            fgrad_ref[s, :, cg * LANES : (cg + 1) * LANES] = tot[cg, s, :taps, :]
    for c in copies:
        c.wait_send()


def shards(streams, filters, out_weight, grad_out, counts, starts):
    _, rows, channels = streams.shape
    taps = filters.shape[1]
    width = grad_out.shape[1]
    g = channels // LANES
    vmem = pl.BlockSpec(memory_space=pltpu.VMEM)
    anywhere = pl.BlockSpec(memory_space=pl.ANY)
    smem = pl.BlockSpec(memory_space=pltpu.SMEM)
    f32, bf16 = jnp.float32, jnp.bfloat16
    V = pltpu.VMEM
    return pl.pallas_call(
        kernel,
        out_shape=(
            jax.ShapeDtypeStruct((3, rows, channels), bf16),
            jax.ShapeDtypeStruct((3, SLOTS, channels), f32),
            jax.ShapeDtypeStruct((3, taps, channels), f32),
        ),
        in_specs=[anywhere, vmem, vmem, anywhere, smem, smem],
        out_specs=(vmem, vmem, vmem),
        scratch_shapes=[
            V((3, rows, channels), bf16),
            V((3, g, rows + 8, LANES), f32),
            V((3, g, rows, LANES), f32),
            V((NZ, NX, NC, 64, channels), bf16),
            V((rows, NY * width), bf16),
            V((g, rows, LANES), f32),
            V((3, g, rows + 8, LANES), f32),
            V((3, g, rows + 2 * TILE, LANES), f32),
            V((3, g, 8, LANES), f32),
            V((3, g, 8, LANES), f32),
            V((3, g, 8, LANES), f32),
            V((3, g, 8, LANES), f32),
            V((3, g, 24, LANES), f32),
            V((SLOTS, 3 * g, LANES), f32),
            V((SLOTS, 3 * g, LANES), f32),
            V((3 * g, LANES), f32),
            V((3 * g, LANES), f32),
            V((3 * g, LANES), f32),
            V((g, 3, 8, LANES), f32),
            V((NG, 3, 8, LANES), f32),
            V((NZ, 3, 8, LANES), f32),
            V((g, 3, 8, LANES), f32),
            pltpu.SemaphoreType.DMA((80,)),
            pltpu.SemaphoreType.DMA((80,)),
            pltpu.SemaphoreType.DMA((2,)),
        ],
        compiler_params=pltpu.CompilerParams(
            collective_id=0, has_side_effects=True, vmem_limit_bytes=60 * 1024 * 1024
        ),
        cost_estimate=pl.CostEstimate(
            flops=2 * rows * channels * NY * width, bytes_accessed=12 * rows * channels, transcendentals=0
        ),
    )(streams, filters, out_weight, grad_out, counts, starts)


def solution(mesh):
    return jax.shard_map(
        shards,
        mesh=mesh,
        in_specs=(
            P(None, "ctx", "tp"),
            P(None, None, "tp"),
            P("tp", "ctx"),
            P("ctx", "tp"),
            P("ctx"),
            P("ctx"),
        ),
        out_specs=(P(None, "ctx", "tp"), P(None, "ctx", "tp"), P(None, None, "tp")),
        check_vma=False,
    )
```

```python
import functools

import jax
import jax.numpy as jnp
from jax import lax
from jax.experimental import pallas as pl
from jax.experimental.pallas import tpu as pltpu
from jax.sharding import PartitionSpec as P

MESH = pl.DeviceIdType.MESH
TILE = 128
LANES = 128
NZ, NX, NC, NY = 8, 4, 2, 8
NG = NX * NC
CH = 64
SLOTS = 4
VLIM = 44


ORDER = (
    "b1", "f", "b2", "a0", "g01", "f", "f", "f", "x0", "f", "b3", "f", "g11", "x1", "A01", "x2",
    "A11", "f", "b4", "g02", "f", "A02", "x3", "g12", "A12", "x4", "A03", "g03", "X", "A13", "g13",
    "A04", "A14",
)


def kernel(
    streams_ref, filters_ref, weight_ref, grad_ref, counts_ref, starts_ref,
    du32, inv_ref, scales_ref, fgrad_ref,
    sv, u32, prod, wt, gg, dc32, tail, halo, head, heads_in, zbuf,
    msc, tmx, max_prev, max_next, fsc, p1, p2,
    send, recv, local,
):
    rows = grad_ref.shape[0]
    width = grad_ref.shape[1]
    taps = filters_ref.shape[1]
    groups = weight_ref.shape[1] // LANES
    i = lax.axis_index("ctx")
    y = lax.axis_index("tp")
    z = i // NG
    q = i % NG
    x = q // NC
    core = q % NC
    n_ctx = NZ * NG

    count = counts_ref[0]
    first = starts_ref[0]
    offset = first % TILE
    last_slot = jnp.clip((offset + count - 1) // TILE, 0, SLOTS - 1)

    def at(zz, xx, cc):
        return ((zz + NZ) % NZ) * NG + ((xx + NX) % NX) * NC + cc

    copies = []

    def push(src, dst, ctx, tp):
        k = len(copies)
        c = pltpu.make_async_remote_copy(
            src_ref=src, dst_ref=dst, send_sem=send.at[k], recv_sem=recv.at[k],
            device_id=(ctx, tp), device_id_type=MESH,
        )
        c.start()
        copies.append(c)
        return c

    up, down = (i + 1) % n_ctx, (i + n_ctx - 1) % n_ctx
    yr, yl = (y + 1) % NY, (y + NY - 1) % NY
    zr, zl = at(z + 1, x, core), at(z - 1, x, core)
    xr, xl = at(z, x + 1, core), at(z, x - 1, core)
    mate = at(z, x, 1 - core)

    get_streams = pltpu.make_async_copy(streams_ref, sv, local.at[0])
    get_streams.start()
    own_cols = pl.ds(pl.multiple_of(y * width, width), width)
    get_grad = pltpu.make_async_copy(grad_ref, gg.at[:, own_cols], local.at[1])
    get_grad.start()

    barrier = pltpu.get_barrier_semaphore()
    peers = [(i, yr), (i, yl), (up, y), (down, y)]
    peers += [(z * NG + (q + d) % NG, y) for d in range(1, NG)]
    peers += [(((z + d) % NZ) * NG + q, y) for d in range(1, NZ)]
    for peer in peers:
        pl.semaphore_signal(barrier, inc=1, device_id=peer, device_id_type=MESH)
    wt[z, x, core] = weight_ref[...]
    pl.semaphore_wait(barrier, len(peers))

    half = rows // 2

    def gblock(c, t):
        t = (t + NY) % NY
        return gg.at[pl.ds(c * half, half), pl.ds(pl.multiple_of(t * width, width), width)]

    def gstep(c, d):
        out = []
        own = grad_ref.at[pl.ds(c * half, half)]
        if d < 4 or c == 0:
            block = gblock(c, y - d + 1)
            out.append(push(own if d == 1 else block, block, i, yr))
        if d < 4 or c == 1:
            block = gblock(c, y + d - 1)
            out.append(push(own if d == 1 else block, block, i, yl))
        return out

    def arrived(cs):
        for c in cs:
            c.wait_recv()

    def ablock(c, zz):
        return wt.at[(zz + NZ) % NZ, pl.ds(2 * c, 2), core, pl.ds(0, 32), :]

    def bpiece(zz, xx, lo=32, n=32):
        return wt.at[(zz + NZ) % NZ, (xx + NX) % NX, core, pl.ds(lo, n), :]

    def bcolumn(xx):
        return wt.at[:, (xx + NX) % NX, core, pl.ds(32, 32), :]

    def same(block, dest):
        return push(block, block, dest, y)

    def astep(c, d):
        out = []
        if d < 4 or c == 0:
            out.append(same(ablock(c, z - d + 1), zr))
        if d < 4 or c == 1:
            out.append(same(ablock(c, z + d - 1), zl))
        return out

    def bstep(d):
        n = 32 if d < 4 else 16
        lo = 32 if d < 4 else 48
        return [same(bpiece(z - d + 1, x, 32, n), zr), same(bpiece(z + d - 1, x, lo, n), zl)]

    def xstep(p):
        out = []
        for zz in [z + p] if p in (0, 4) else [z + p, z - p]:
            out += [same(bpiece(zz, x), xr), same(bpiece(zz, x), xl)]
        return out

    flight = {"X": []}
    mates = []
    own = wt.at[z, x, core, pl.ds(0, 32), :]
    flight["g01"] = gstep(0, 1)
    flight["a0"] = [same(own, at(z, x + d, core)) for d in range(1, NX)]
    flight["b1"] = bstep(1)
    flight["x0"] = xstep(0)
    flight["g11"] = gstep(1, 1)

    get_streams.wait()

    def widen(cg, _):
        lanes = pl.ds(pl.multiple_of(cg * LANES, LANES), LANES)
        for s in range(3):
            u32[s, cg, 8 : 8 + rows, :] = sv[s, :, lanes].astype(jnp.float32)
            tail[s, cg] = u32[s, cg, pl.ds(jnp.clip(count, 8, rows), 8), :]
        return 0

    lax.fori_loop(0, groups, widen, 0)
    tails = push(tail, halo, up, y)

    def forward(cg):
        lanes = pl.ds(pl.multiple_of(cg * LANES, LANES), LANES)
        coef = []
        for s in range(3):
            u32[s, cg, 0:8, :] = jnp.where(i > 0, halo[s, cg], 0.0)
            du32[s, cg, 0:TILE, :] = jnp.zeros((TILE, LANES), jnp.float32)
            du32[s, cg, TILE + rows :, :] = jnp.zeros((TILE, LANES), jnp.float32)
            dc32[s, cg, rows:, :] = jnp.zeros((8, LANES), jnp.float32)
            zbuf[s, cg] = jnp.zeros((24, LANES), jnp.float32)
            coef.append([filters_ref[s, pl.ds(j, 1), lanes] for j in range(taps)])

        def chunk(r, _):
            r0 = pl.multiple_of(r * CH, CH)
            c = []
            for s in range(3):
                acc = coef[s][0] * u32[s, cg, pl.ds(8 + r0, CH), :]
                for j in range(1, taps):
                    acc = acc + coef[s][j] * u32[s, cg, pl.ds(8 + r0 - j, CH), :]
                c.append(acc)
            prod[0, cg, pl.ds(r0, CH), :] = c[1] * c[2]
            prod[1, cg, pl.ds(r0, CH), :] = c[0] * c[2]
            prod[2, cg, pl.ds(r0, CH), :] = c[0] * c[1]
            return 0

        lax.fori_loop(0, rows // CH, chunk, 0)

    done = 0
    for token in ORDER:
        kind = token[0]
        if kind == "f":
            if done == 0:
                tails.wait_recv()
            forward(done)
            done += 1
            continue
        arrived(flight[token])
        if kind == "g" or kind == "A":
            c, d = int(token[1]), int(token[2])
            if d < 4:
                flight[f"{kind}{c}{d + 1}"] = (gstep if kind == "g" else astep)(c, d + 1)
            if kind == "A":
                mates.append(same(ablock(c, z - d), mate))
                if d < 4:
                    mates.append(same(ablock(c, z + d), mate))
        elif kind == "a":
            flight["A01"], flight["A11"] = astep(0, 1), astep(1, 1)
            mates += [same(ablock(0, z), mate), same(ablock(1, z), mate)]
        elif kind == "b":
            d = int(token[1])
            if d < 4:
                flight[f"b{d + 1}"] = bstep(d + 1)
            else:
                mates.append(same(bcolumn(x), mate))
            flight[f"x{d}"] = xstep(d)
        elif kind == "x":
            p = int(token[1])
            if p < 4:
                flight["X"].append(same(bpiece(z + p, x - 1), xr))
            if p > 0:
                flight["X"].append(same(bpiece(z - p, x + 1), xl))
            if p == 4:
                mates += [same(bcolumn(x - 1), mate), same(bcolumn(x + 1), mate)]
        else:
            mates.append(same(bcolumn(x + 2), mate))
    get_grad.wait()
    arrived(mates)

    def project(c):
        def block(n, _):
            cols = pl.ds(pl.multiple_of(n * 256, 256), 256)
            w = wt[:, :, :, :, cols].reshape(NZ * NG * 64, 256)
            dy = jnp.dot(gg[pl.ds(c * half, half), :], w, preferred_element_type=jnp.float32)
            for r in range(c * half, (c + 1) * half, CH):
                live = lax.broadcasted_iota(jnp.int32, (CH, LANES), 0) + r < count
                for e in range(2):
                    part = dy[r - c * half : r - c * half + CH, e * LANES : (e + 1) * LANES]
                    part = part.astype(jnp.bfloat16).astype(jnp.float32)
                    for s in range(3):
                        dc = jnp.where(live, part * prod[s, 2 * n + e, r : r + CH, :], 0.0)
                        dc32[s, 2 * n + e, r : r + CH, :] = dc.astype(jnp.bfloat16).astype(jnp.float32)
            return 0

        lax.fori_loop(0, groups // 2, block, 0)

    def correlate(c):
        def group(cg, _):
            for s in range(3):
                acc = [jnp.zeros((8, LANES), jnp.float32)] * taps
                for r in range(c * half, (c + 1) * half, CH):
                    dc = dc32[s, cg, r : r + CH, :]
                    for j in range(taps):
                        term = dc * u32[s, cg, 8 + r - j : 8 + r - j + CH, :]
                        acc[j] = acc[j] + term.reshape(CH // 8, 8, LANES).sum(0)
                if c == 0:
                    fsc[cg, s] = jnp.zeros((8, LANES), jnp.float32)
                for j in range(taps):
                    term = acc[j].sum(0, keepdims=True)
                    if c == 1:
                        term = term + fsc[cg, s, j : j + 1, :]
                    fsc[cg, s, j : j + 1, :] = term
            return 0

        lax.fori_loop(0, groups, group, 0)

    arrived(flight["g04"])
    project(0)
    head[...] = dc32[:, :, 0:8, :]
    heads = push(head, heads_in, down, y)
    correlate(0)
    arrived(flight["g14"])
    project(1)
    correlate(1)
    f1 = []
    for d in range(1, NG):
        to = (q + d) % NG
        f1.append(push(fsc.at[to], p1.at[d], z * NG + to, y))

    heads.wait_recv()

    def backward(cg, _):
        lanes = pl.ds(pl.multiple_of(cg * LANES, LANES), LANES)
        for s in range(3):
            zbuf[s, cg, 8:16, :] = jnp.where(i < n_ctx - 1, heads_in[s, cg], 0.0)

        def insert(r, _):
            r0 = pl.multiple_of(r * 8, 8)
            at_row = jnp.clip(r0 - count, -8, 8) + 8
            for s in range(3):
                dc32[s, cg, pl.ds(r0, 8), :] += zbuf[s, cg, pl.ds(at_row, 8), :]
            return 0

        lax.fori_loop(rows // 16, rows // 8 + 1, insert, 0)
        coef = [[filters_ref[s, pl.ds(j, 1), lanes] for j in range(taps)] for s in range(3)]

        for r in range(0, rows, CH):
            live = lax.broadcasted_iota(jnp.int32, (CH, LANES), 0) + r < count
            for s in range(3):
                acc = coef[s][0] * dc32[s, cg, r : r + CH, :]
                for j in range(1, taps):
                    acc = acc + coef[s][j] * dc32[s, cg, r + j : r + j + CH, :]
                du32[s, cg, TILE + r : TILE + r + CH, :] = jnp.where(live, acc, 0.0)

        for s in range(3):
            for k in range(SLOTS):
                block = jnp.abs(du32[s, cg, pl.ds((k + 1) * TILE - offset, TILE), :])
                top = block.reshape(TILE // 8, 8, LANES).max(0).max(0, keepdims=True)
                msc[k, pl.ds(s * groups + cg, 1), :] = top
        return 0

    lax.fori_loop(0, groups // 2, backward, 0)
    arrived(f1)
    part = fsc[q]
    for d in range(1, NG):
        part = part + p1[d]
    p2[z] = part
    f2 = []
    for d in range(1, NZ):
        f2.append(push(p2.at[z], p2.at[z], ((z + d) % NZ) * NG + q, y))
    lax.fori_loop(groups // 2, groups, backward, 0)
    tmx[...] = msc[last_slot]
    to_next = push(tmx, max_prev, up, y)
    to_prev = push(msc.at[0], max_next, down, y)

    arrived(f2)
    total = p2[0]
    for d in range(1, NZ):
        total = total + p2[d]
    fgrad_ref[q] = total
    f3 = []
    for d in range(1, NG):
        f3.append(push(fgrad_ref.at[q], fgrad_ref.at[q], z * NG + (q + d) % NG, y))

    to_next.wait_recv()
    to_prev.wait_recv()
    prev = jnp.where(offset != 0, max_prev[...], 0.0)
    follow = jnp.where((first + count) % TILE != 0, max_next[...], 0.0)
    for k in range(SLOTS):
        top = msc[k]
        if k == 0:
            top = jnp.maximum(top, prev)
        top = jnp.maximum(top, jnp.where(last_slot == k, follow, 0.0))
        scale = top + 1e-6
        inv_ref[k] = 1.0 / scale
        scales_ref[k] = jnp.where(last_slot >= k, scale, 0.0)

    arrived(f3)
    for c in copies:
        c.wait_send()


def finish(starts_ref, du_ref, inv_ref, scale_ref, fgrad_ref, pay_out, scales_out, fgrad_out):
    s = pl.program_id(0)
    groups, rows = du_ref.shape[1], pay_out.shape[1]
    offset = starts_ref[0] % TILE
    taps = fgrad_out.shape[1]

    def group(cg, _):
        lanes = pl.ds(pl.multiple_of(cg * LANES, LANES), LANES)
        row = pl.ds(s * groups + cg, 1)
        inv = [inv_ref[k, row, :] for k in range(SLOTS)]
        for k in range(SLOTS):
            scales_out[0, k : k + 1, lanes] = scale_ref[k, row, :]
        fgrad_out[0, :, lanes] = fgrad_ref[cg, s, :taps, :]
        for r in range(0, rows, CH):
            pos = lax.broadcasted_iota(jnp.int32, (CH, LANES), 0) + (r + offset)
            scale = jnp.where(pos >= 3 * TILE, inv[3], inv[2])
            scale = jnp.where(pos >= 2 * TILE, scale, inv[1])
            scale = jnp.where(pos >= TILE, scale, inv[0])
            du = du_ref[s, cg, TILE + r : TILE + r + CH, :]
            pay_out[0, r : r + CH, lanes] = (du * scale).astype(jnp.bfloat16)
        return 0

    lax.fori_loop(0, groups, group, 0)


def shards(streams, filters, out_weight, grad_out, counts, starts):
    _, rows, channels = streams.shape
    taps = filters.shape[1]
    width = grad_out.shape[1]
    g = channels // LANES
    vmem = pl.BlockSpec(memory_space=pltpu.VMEM)
    anywhere = pl.BlockSpec(memory_space=pl.ANY)
    smem = pl.BlockSpec(memory_space=pltpu.SMEM)
    f32, bf16 = jnp.float32, jnp.bfloat16
    V = pltpu.VMEM
    du, inv, scale, fgrad = pl.pallas_call(
        kernel,
        out_shape=(
            V((3, g, rows + 2 * TILE, LANES), f32),
            V((SLOTS, 3 * g, LANES), f32),
            V((SLOTS, 3 * g, LANES), f32),
            V((NG, 3, 8, LANES), f32),
        ),
        in_specs=[anywhere, vmem, vmem, anywhere, smem, smem],
        out_specs=(vmem, vmem, vmem, vmem),
        scratch_shapes=[
            V((3, rows, channels), bf16),
            V((3, g, rows + 8, LANES), f32),
            V((3, g, rows, LANES), f32),
            V((NZ, NX, NC, 64, channels), bf16),
            V((rows, NY * width), bf16),
            V((3, g, rows + 8, LANES), f32),
            V((3, g, 8, LANES), f32),
            V((3, g, 8, LANES), f32),
            V((3, g, 8, LANES), f32),
            V((3, g, 8, LANES), f32),
            V((3, g, 24, LANES), f32),
            V((SLOTS, 3 * g, LANES), f32),
            V((3 * g, LANES), f32),
            V((3 * g, LANES), f32),
            V((3 * g, LANES), f32),
            V((g, 3, 8, LANES), f32),
            V((NG, 3, 8, LANES), f32),
            V((NZ, 3, 8, LANES), f32),
            pltpu.SemaphoreType.DMA((128,)),
            pltpu.SemaphoreType.DMA((128,)),
            pltpu.SemaphoreType.DMA((2,)),
        ],
        compiler_params=pltpu.CompilerParams(
            collective_id=0, has_side_effects=True, vmem_limit_bytes=VLIM * 1024 * 1024
        ),
        cost_estimate=pl.CostEstimate(
            flops=2 * rows * channels * NY * width, bytes_accessed=12 * rows * channels, transcendentals=0
        ),
    )(streams, filters, out_weight.T, grad_out, counts, starts)
    return pl.pallas_call(
        finish,
        grid=(3,),
        out_shape=(
            jax.ShapeDtypeStruct((3, rows, channels), bf16),
            jax.ShapeDtypeStruct((3, SLOTS, channels), f32),
            jax.ShapeDtypeStruct((3, taps, channels), f32),
        ),
        in_specs=[smem, vmem, vmem, vmem, vmem],
        out_specs=(
            pl.BlockSpec((1, rows, channels), lambda s: (s, 0, 0)),
            pl.BlockSpec((1, SLOTS, channels), lambda s: (s, 0, 0)),
            pl.BlockSpec((1, taps, channels), lambda s: (s, 0, 0)),
        ),
        compiler_params=pltpu.CompilerParams(vmem_limit_bytes=20 * 1024 * 1024),
    )(starts, du, inv, scale, fgrad)


def solution(mesh):
    return jax.shard_map(
        shards,
        mesh=mesh,
        in_specs=(
            P(None, "ctx", "tp"),
            P(None, None, "tp"),
            P("tp", "ctx"),
            P("ctx", "tp"),
            P("ctx"),
            P("ctx"),
        ),
        out_specs=(P(None, "ctx", "tp"), P(None, "ctx", "tp"), P(None, None, "tp")),
        check_vma=False,
    )
```

```python
import functools

import jax
import jax.numpy as jnp
from jax import lax
from jax.experimental import pallas as pl
from jax.experimental.pallas import tpu as pltpu
from jax.sharding import PartitionSpec as P

MESH = pl.DeviceIdType.MESH
TILE = 128
LANES = 128
NZ, NX, NC, NY = 8, 4, 2, 8
NG = NX * NC
CH = 64
SLOTS = 4
VLIM = 54


ORDER = (
    "b01", "g001", "a0", "b02", "f", "x00", "f", "f", "f", "g011", "x01", "f", "f", "f", "x02",
    "f", "A01", "g002", "b03", "g012", "x03", "A02", "b04", "g003", "b11", "a1", "x10", "g013",
    "x04", "A03", "b12", "g004", "x11", "X0", "g014", "g101", "x12", "A11", "A04", "g111", "b13",
    "P0", "g102", "x13", "A12", "P1", "b14", "g112", "x14", "g103", "A13", "X1", "Q0", "g113",
    "A14", "P2", "P3", "Q1",
)


def kernel(
    streams_ref, filters_ref, weight_ref, grad_ref, counts_ref, starts_ref,
    du32, inv_ref, scales_ref, fgrad_ref,
    sv, fv, u32, prod, wt, gg, dyb, dc32, tail, halo, head, heads_in, zbuf,
    msc, tmx, max_prev, max_next, facc, fsc, p1, p2,
    send, recv, local,
):
    rows = grad_ref.shape[0]
    width = grad_ref.shape[1]
    taps = filters_ref.shape[1]
    groups = weight_ref.shape[1] // LANES
    i = lax.axis_index("ctx")
    y = lax.axis_index("tp")
    z = i // NG
    q = i % NG
    x = q // NC
    core = q % NC
    n_ctx = NZ * NG

    count = counts_ref[0]
    first = starts_ref[0]
    offset = first % TILE
    last_slot = jnp.clip((offset + count - 1) // TILE, 0, SLOTS - 1)

    def at(zz, xx, cc):
        return ((zz + NZ) % NZ) * NG + ((xx + NX) % NX) * NC + cc

    copies = []

    def push(src, dst, ctx, tp):
        k = len(copies)
        c = pltpu.make_async_remote_copy(
            src_ref=src, dst_ref=dst, send_sem=send.at[k], recv_sem=recv.at[k],
            device_id=(ctx, tp), device_id_type=MESH,
        )
        c.start()
        copies.append(c)
        return c

    up, down = (i + 1) % n_ctx, (i + n_ctx - 1) % n_ctx
    yr, yl = (y + 1) % NY, (y + NY - 1) % NY
    zr, zl = at(z + 1, x, core), at(z - 1, x, core)
    xr, xl = at(z, x + 1, core), at(z, x - 1, core)
    mate = at(z, x, 1 - core)

    get_streams = pltpu.make_async_copy(streams_ref, sv, local.at[0])
    get_streams.start()
    own_cols = pl.ds(pl.multiple_of(y * width, width), width)
    get_grad = pltpu.make_async_copy(grad_ref, gg.at[:, own_cols], local.at[1])
    get_grad.start()

    get_weight = pltpu.make_async_copy(weight_ref, wt.at[z, x, core], local.at[2])
    get_weight.start()
    get_filters = pltpu.make_async_copy(filters_ref, fv, local.at[3])
    get_filters.start()

    barrier = pltpu.get_barrier_semaphore()
    peers = [(i, yr), (i, yl), (up, y), (down, y)]
    peers += [(z * NG + (q + d) % NG, y) for d in range(1, NG)]
    peers += [(((z + d) % NZ) * NG + q, y) for d in range(1, NZ)]
    for peer in peers:
        pl.semaphore_signal(barrier, inc=1, device_id=peer, device_id_type=MESH)
    pl.semaphore_wait(barrier, len(peers))

    half = rows // 2
    quarter = half // 2

    def gblock(c, u, t):
        t = (t + NY) % NY
        cols = pl.ds(pl.multiple_of(t * width, width), width)
        return gg.at[pl.ds(c * half + u * quarter, quarter), cols]

    def gstep(c, u, d):
        out = []
        own = grad_ref.at[pl.ds(c * half + u * quarter, quarter)]
        if d < 4 or u == 0:
            block = gblock(c, u, y - d + 1)
            out.append(push(own if d == 1 else block, block, i, yr))
        if d < 4 or u == 1:
            block = gblock(c, u, y + d - 1)
            out.append(push(own if d == 1 else block, block, i, yl))
        return out

    def arrived(cs):
        for c in cs:
            c.wait_recv()

    span = groups * LANES // 2

    def ablock(n, zz, lo=0, many=NX):
        return wt.at[(zz + NZ) % NZ, pl.ds(lo, many), core, pl.ds(0, 32), pl.ds(n * span, span)]

    def bpiece(n, zz, xx, lo=32, many=32):
        return wt.at[(zz + NZ) % NZ, (xx + NX) % NX, core, pl.ds(lo, many), pl.ds(n * span, span)]

    def bcolumn(n, xx):
        return wt.at[:, (xx + NX) % NX, core, pl.ds(32, 32), pl.ds(n * span, span)]

    def same(block, dest):
        return push(block, block, dest, y)

    def astep(n, d):
        many = NX if d < 4 else NX // 2
        lo = NX - many
        return [same(ablock(n, z - d + 1, 0, many), zr), same(ablock(n, z + d - 1, lo, many), zl)]

    def bstep(n, d):
        many = 32 if d < 4 else 16
        lo = 64 - many
        return [same(bpiece(n, z - d + 1, x, 32, many), zr), same(bpiece(n, z + d - 1, x, lo, many), zl)]

    def xstep(n, p):
        out = []
        for zz in [z + p] if p in (0, 4) else [z + p, z - p]:
            out += [same(bpiece(n, zz, x), xr), same(bpiece(n, zz, x), xl)]
        return out

    def wstart(n):
        own = wt.at[z, x, core, pl.ds(0, 32), pl.ds(n * span, span)]
        flight[f"a{n}"] = [same(own, at(z, x + d, core)) for d in range(1, NX)]
        flight[f"b{n}1"] = bstep(n, 1)
        flight[f"x{n}0"] = xstep(n, 0)

    flight = {"X0": [], "X1": []}
    mates = [[], []]
    flight["g001"] = gstep(0, 0, 1)
    get_weight.wait()
    wstart(0)
    flight["g011"] = gstep(0, 1, 1)

    get_streams.wait()

    def widen(cg, _):
        lanes = pl.ds(pl.multiple_of(cg * LANES, LANES), LANES)
        for s in range(3):
            u32[s, cg, 8 : 8 + rows, :] = sv[s, :, lanes].astype(jnp.float32)
            tail[s, cg] = u32[s, cg, pl.ds(jnp.clip(count, 8, rows), 8), :]
        return 0

    lax.fori_loop(0, groups, widen, 0)
    tails = push(tail, halo, up, y)

    def forward(cg):
        lanes = pl.ds(pl.multiple_of(cg * LANES, LANES), LANES)
        coef = []
        for s in range(3):
            u32[s, cg, 0:8, :] = jnp.where(i > 0, halo[s, cg], 0.0)
            du32[s, cg, 0:TILE, :] = jnp.zeros((TILE, LANES), jnp.float32)
            du32[s, cg, TILE + rows :, :] = jnp.zeros((TILE, LANES), jnp.float32)
            dc32[s, cg, rows:, :] = jnp.zeros((8, LANES), jnp.float32)
            zbuf[s, cg] = jnp.zeros((24, LANES), jnp.float32)
            for k in range(taps, 8):
                fsc[cg, s, k : k + 1, :] = jnp.zeros((1, LANES), jnp.float32)
            coef.append([fv[s, pl.ds(j, 1), lanes] for j in range(taps)])

        def chunk(r, _):
            r0 = pl.multiple_of(r * CH, CH)
            c = []
            for s in range(3):
                acc = coef[s][0] * u32[s, cg, pl.ds(8 + r0, CH), :]
                for j in range(1, taps):
                    acc = acc + coef[s][j] * u32[s, cg, pl.ds(8 + r0 - j, CH), :]
                c.append(acc)
            prod[0, cg, pl.ds(r0, CH), :] = c[1] * c[2]
            prod[1, cg, pl.ds(r0, CH), :] = c[0] * c[2]
            prod[2, cg, pl.ds(r0, CH), :] = c[0] * c[1]
            return 0

        lax.fori_loop(0, rows // CH, chunk, 0)

    def project(c, b, slot):
        cols = pl.ds(pl.multiple_of(b * 256, 256), 256)
        w = wt[:, :, :, :, cols].reshape(NZ * NG * 64, 256)
        dy = jnp.dot(gg[pl.ds(c * half, half), :], w, preferred_element_type=jnp.float32)
        dyb[slot] = dy.astype(jnp.bfloat16).astype(jnp.float32)

    def gate(c, b, slot):
        for r in range(c * half, (c + 1) * half, CH):
            live = lax.broadcasted_iota(jnp.int32, (CH, LANES), 0) + r < count
            for e in range(2):
                dy = dyb[slot, r - c * half : r - c * half + CH, e * LANES : (e + 1) * LANES]
                for s in range(3):
                    dc = jnp.where(live, dy * prod[s, 2 * b + e, r : r + CH, :], 0.0)
                    dc32[s, 2 * b + e, r : r + CH, :] = dc.astype(jnp.bfloat16).astype(jnp.float32)
        for e in range(2):
            cg = 2 * b + e
            for s in range(3):
                if c == 0:
                    acc = [jnp.zeros((8, LANES), jnp.float32)] * taps
                    head[s, cg] = dc32[s, cg, 0:8, :]
                else:
                    acc = [facc[cg, s, j] for j in range(taps)]
                for r in range(c * half, (c + 1) * half, CH):
                    dc = dc32[s, cg, r : r + CH, :]
                    for j in range(taps):
                        term = dc * u32[s, cg, 8 + r - j : 8 + r - j + CH, :]
                        acc[j] = acc[j] + term.reshape(CH // 8, 8, LANES).sum(0)
                for j in range(taps):
                    if c == 0:
                        facc[cg, s, j] = acc[j]
                    else:
                        fsc[cg, s, j : j + 1, :] = acc[j].sum(0, keepdims=True)

    def rows_back(cg, lo, hi):
        lanes = pl.ds(pl.multiple_of(cg * LANES, LANES), LANES)
        coef = [[fv[s, pl.ds(j, 1), lanes] for j in range(taps)] for s in range(3)]
        for r in range(lo, hi, CH):
            live = lax.broadcasted_iota(jnp.int32, (CH, LANES), 0) + r < count
            for s in range(3):
                acc = coef[s][0] * dc32[s, cg, r : r + CH, :]
                for j in range(1, taps):
                    acc = acc + coef[s][j] * dc32[s, cg, r + j : r + j + CH, :]
                du32[s, cg, TILE + r : TILE + r + CH, :] = jnp.where(live, acc, 0.0)

    early = (half - 8) // CH * CH

    def first_rows(cg, _):
        rows_back(cg, 0, early)
        return 0

    done = 0
    for token in ORDER:
        kind = token[0]
        if kind == "f":
            if done == 0:
                get_filters.wait()
                tails.wait_recv()
            forward(done)
            done += 1
            continue
        n = int(token[1])
        if kind == "P":
            if n == 0:
                get_grad.wait()
            if n % 2 == 0:
                arrived(mates[n // 2])
            project(0, n, 0)
            gate(0, n, 0)
            continue
        if kind == "Q":
            lax.fori_loop(n * groups // 2, (n + 1) * groups // 2, first_rows, 0)
            continue
        arrived(flight[token])
        if kind == "g":
            u, d = int(token[2]), int(token[3])
            if d < 4:
                flight[f"g{n}{u}{d + 1}"] = gstep(n, u, d + 1)
            if d == 3 and n == 0:
                flight[f"g1{u}1"] = gstep(1, u, 1)
        elif kind == "A":
            d = int(token[2])
            if d < 4:
                flight[f"A{n}{d + 1}"] = astep(n, d + 1)
                mates[n].append(same(ablock(n, z + d), mate))
            mates[n].append(same(ablock(n, z - d), mate))
        elif kind == "a":
            flight[f"A{n}1"] = astep(n, 1)
            mates[n].append(same(ablock(n, z), mate))
        elif kind == "b":
            d = int(token[2])
            if d < 4:
                flight[f"b{n}{d + 1}"] = bstep(n, d + 1)
            flight[f"x{n}{d}"] = xstep(n, d)
            if d == 4:
                mates[n].append(same(bcolumn(n, x), mate))
            if n == 0 and d == 3:
                wstart(1)
        elif kind == "x":
            p = int(token[2])
            if p < 4:
                flight[f"X{n}"].append(same(bpiece(n, z + p, x - 1), xr))
            if p > 0:
                flight[f"X{n}"].append(same(bpiece(n, z - p, x + 1), xl))
            if p == 4:
                mates[n] += [same(bcolumn(n, x - 1), mate), same(bcolumn(n, x + 1), mate)]
        else:
            mates[n].append(same(bcolumn(n, x + 2), mate))

    heads = push(head, heads_in, down, y)
    arrived(flight["g104"])
    arrived(flight["g114"])
    project(1, 0, 0)

    def both(b, _):
        gate(1, b - 1, (b - 1) % 2)
        project(1, b, b % 2)
        return 0

    lax.fori_loop(1, groups // 2, both, 0)
    gate(1, groups // 2 - 1, (groups // 2 - 1) % 2)
    f1 = []
    for d in range(1, NG):
        to = (q + d) % NG
        f1.append(push(fsc.at[to], p1.at[d], z * NG + to, y))

    heads.wait_recv()

    def backward(cg, _):
        for s in range(3):
            zbuf[s, cg, 8:16, :] = jnp.where(i < n_ctx - 1, heads_in[s, cg], 0.0)

        def insert(r, _):
            r0 = pl.multiple_of(r * 8, 8)
            at_row = jnp.clip(r0 - count, -8, 8) + 8
            for s in range(3):
                dc32[s, cg, pl.ds(r0, 8), :] += zbuf[s, cg, pl.ds(at_row, 8), :]
            return 0

        lax.fori_loop(half // 8, rows // 8 + 1, insert, 0)
        rows_back(cg, early, rows)

        for s in range(3):
            for k in range(SLOTS):
                block = jnp.abs(du32[s, cg, pl.ds((k + 1) * TILE - offset, TILE), :])
                top = block.reshape(TILE // 8, 8, LANES).max(0).max(0, keepdims=True)
                msc[k, pl.ds(s * groups + cg, 1), :] = top
        return 0

    lax.fori_loop(0, groups // 2, backward, 0)
    arrived(f1)
    part = fsc[q]
    for d in range(1, NG):
        part = part + p1[d]
    p2[z] = part
    f2 = []
    for d in range(1, NZ):
        f2.append(push(p2.at[z], p2.at[z], ((z + d) % NZ) * NG + q, y))
    lax.fori_loop(groups // 2, groups, backward, 0)
    tmx[...] = msc[last_slot]
    to_next = push(tmx, max_prev, up, y)
    to_prev = push(msc.at[0], max_next, down, y)

    arrived(f2)
    total = p2[0]
    for d in range(1, NZ):
        total = total + p2[d]
    fgrad_ref[q] = total
    f3 = []
    for d in range(1, NG):
        f3.append(push(fgrad_ref.at[q], fgrad_ref.at[q], z * NG + (q + d) % NG, y))

    to_next.wait_recv()
    to_prev.wait_recv()
    prev = jnp.where(offset != 0, max_prev[...], 0.0)
    follow = jnp.where((first + count) % TILE != 0, max_next[...], 0.0)
    for k in range(SLOTS):
        top = msc[k]
        if k == 0:
            top = jnp.maximum(top, prev)
        top = jnp.maximum(top, jnp.where(last_slot == k, follow, 0.0))
        scale = top + 1e-6
        inv_ref[k] = 1.0 / scale
        scales_ref[k] = jnp.where(last_slot >= k, scale, 0.0)

    arrived(f3)
    for c in copies:
        c.wait_send()


def finish(starts_ref, du_ref, inv_ref, scale_ref, fgrad_ref, pay_out, scales_out, fgrad_out):
    s = pl.program_id(0)
    groups, rows = du_ref.shape[1], pay_out.shape[1]
    base = pl.program_id(1) * rows
    offset = starts_ref[0] % TILE
    taps = fgrad_out.shape[1]

    def group(cg, _):
        lanes = pl.ds(pl.multiple_of(cg * LANES, LANES), LANES)
        row = pl.ds(s * groups + cg, 1)
        inv = [inv_ref[k, row, :] for k in range(SLOTS)]
        for k in range(SLOTS):
            scales_out[0, k : k + 1, lanes] = scale_ref[k, row, :]
        fgrad_out[0, :, lanes] = fgrad_ref[cg, s, :taps, :]
        for r in range(0, rows, CH):
            pos = lax.broadcasted_iota(jnp.int32, (CH, LANES), 0) + (base + r + offset)
            scale = jnp.where(pos >= 3 * TILE, inv[3], inv[2])
            scale = jnp.where(pos >= 2 * TILE, scale, inv[1])
            scale = jnp.where(pos >= TILE, scale, inv[0])
            du = du_ref[s, cg, pl.ds(pl.multiple_of(TILE + base + r, CH), CH), :]
            pay_out[0, r : r + CH, lanes] = (du * scale).astype(jnp.bfloat16)
        return 0

    lax.fori_loop(0, groups, group, 0)


def shards(streams, filters, out_weight, grad_out, counts, starts):
    _, rows, channels = streams.shape
    taps = filters.shape[1]
    width = grad_out.shape[1]
    g = channels // LANES
    vmem = pl.BlockSpec(memory_space=pltpu.VMEM)
    smem = pl.BlockSpec(memory_space=pltpu.SMEM)
    hbm = pl.BlockSpec(memory_space=pltpu.HBM)
    f32, bf16 = jnp.float32, jnp.bfloat16
    V = pltpu.VMEM
    du, inv, scale, fgrad = pl.pallas_call(
        kernel,
        out_shape=(
            V((3, g, rows + 2 * TILE, LANES), f32),
            V((SLOTS, 3 * g, LANES), f32),
            V((SLOTS, 3 * g, LANES), f32),
            V((NG, 3, 8, LANES), f32),
        ),
        in_specs=[hbm, hbm, hbm, hbm, smem, smem],
        out_specs=(vmem, vmem, vmem, vmem),
        scratch_shapes=[
            V((3, rows, channels), bf16),
            V((3, taps, channels), f32),
            V((3, g, rows + 8, LANES), f32),
            V((3, g, rows, LANES), f32),
            V((NZ, NX, NC, 64, channels), bf16),
            V((rows, NY * width), bf16),
            V((2, rows // 2, 256), f32),
            V((3, g, rows + 8, LANES), f32),
            V((3, g, 8, LANES), f32),
            V((3, g, 8, LANES), f32),
            V((3, g, 8, LANES), f32),
            V((3, g, 8, LANES), f32),
            V((3, g, 24, LANES), f32),
            V((SLOTS, 3 * g, LANES), f32),
            V((3 * g, LANES), f32),
            V((3 * g, LANES), f32),
            V((3 * g, LANES), f32),
            V((g, 3, 8, 8, LANES), f32),
            V((g, 3, 8, LANES), f32),
            V((NG, 3, 8, LANES), f32),
            V((NZ, 3, 8, LANES), f32),
            pltpu.SemaphoreType.DMA((176,)),
            pltpu.SemaphoreType.DMA((176,)),
            pltpu.SemaphoreType.DMA((4,)),
        ],
        compiler_params=pltpu.CompilerParams(
            collective_id=0, has_side_effects=True, vmem_limit_bytes=VLIM * 1024 * 1024
        ),
        cost_estimate=pl.CostEstimate(
            flops=2 * rows * channels * NY * width, bytes_accessed=12 * rows * channels, transcendentals=0
        ),
    )(streams, filters, out_weight.T, grad_out, counts, starts)
    return pl.pallas_call(
        finish,
        grid=(3, 2),
        out_shape=(
            jax.ShapeDtypeStruct((3, rows, channels), bf16),
            jax.ShapeDtypeStruct((3, SLOTS, channels), f32),
            jax.ShapeDtypeStruct((3, taps, channels), f32),
        ),
        in_specs=[smem, vmem, vmem, vmem, vmem],
        out_specs=(
            pl.BlockSpec((1, rows // 2, channels), lambda s, h: (s, h, 0)),
            pl.BlockSpec((1, SLOTS, channels), lambda s, h: (s, 0, 0)),
            pl.BlockSpec((1, taps, channels), lambda s, h: (s, 0, 0)),
        ),
        compiler_params=pltpu.CompilerParams(vmem_limit_bytes=20 * 1024 * 1024),
    )(starts, du, inv, scale, fgrad)


def solution(mesh):
    return jax.shard_map(
        shards,
        mesh=mesh,
        in_specs=(
            P(None, "ctx", "tp"),
            P(None, None, "tp"),
            P("tp", "ctx"),
            P("ctx", "tp"),
            P("ctx"),
            P("ctx"),
        ),
        out_specs=(P(None, "ctx", "tp"), P(None, "ctx", "tp"), P(None, None, "tp")),
        check_vma=False,
    )
```

```python
import functools

import jax
import jax.numpy as jnp
from jax import lax
from jax.experimental import pallas as pl
from jax.experimental.pallas import tpu as pltpu
from jax.sharding import PartitionSpec as P

MESH = pl.DeviceIdType.MESH
TILE = 128
LANES = 128
NZ, NX, NC, NY = 8, 4, 2, 8
NG = NX * NC
CH = 64
SLOTS = 4
VLIM = 54


ORDER = (
    "b1", "b2", "g01", "a0", "b3", "b4", "f", "g11", "f", "f", "A01", "f", "g02", "A11", "x0",
    "A02", "g12", "A12", "x1", "g03", "A03", "A13", "g13", "X", "A04", "A14",
)


def kernel(
    streams_ref, filters_ref, weight_ref, grad_ref, counts_ref, starts_ref,
    du32, inv_ref, scales_ref, fgrad_ref,
    sv, fv, u32, prod, wt, gg, dyb, dc32, tail, halo, head, heads_in, zbuf,
    msc, tmx, max_prev, max_next, fsc, p1, p2,
    send, recv, local,
):
    rows = grad_ref.shape[0]
    width = grad_ref.shape[1]
    taps = filters_ref.shape[1]
    groups = weight_ref.shape[1] // LANES
    i = lax.axis_index("ctx")
    y = lax.axis_index("tp")
    z = i // NG
    q = i % NG
    x = q // NC
    core = q % NC
    n_ctx = NZ * NG

    count = counts_ref[0]
    first = starts_ref[0]
    offset = first % TILE
    last_slot = jnp.clip((offset + count - 1) // TILE, 0, SLOTS - 1)

    def at(zz, xx, cc):
        return ((zz + NZ) % NZ) * NG + ((xx + NX) % NX) * NC + cc

    copies = []

    def push(src, dst, ctx, tp):
        k = len(copies)
        c = pltpu.make_async_remote_copy(
            src_ref=src, dst_ref=dst, send_sem=send.at[k], recv_sem=recv.at[k],
            device_id=(ctx, tp), device_id_type=MESH,
        )
        c.start()
        copies.append(c)
        return c

    up, down = (i + 1) % n_ctx, (i + n_ctx - 1) % n_ctx
    yr, yl = (y + 1) % NY, (y + NY - 1) % NY
    zr, zl = at(z + 1, x, core), at(z - 1, x, core)
    xr, xl = at(z, x + 1, core), at(z, x - 1, core)
    mate = at(z, x, 1 - core)

    get_streams = pltpu.make_async_copy(streams_ref, sv, local.at[0])
    get_streams.start()
    own_cols = pl.ds(pl.multiple_of(y * width, width), width)
    get_grad = pltpu.make_async_copy(grad_ref, gg.at[:, own_cols], local.at[1])
    get_grad.start()

    get_weight = pltpu.make_async_copy(weight_ref, wt.at[z, x, core], local.at[2])
    get_weight.start()
    get_filters = pltpu.make_async_copy(filters_ref, fv, local.at[3])
    get_filters.start()

    barrier = pltpu.get_barrier_semaphore()
    peers = [(i, yr), (i, yl), (up, y), (down, y)]
    peers += [(z * NG + (q + d) % NG, y) for d in range(1, NG)]
    peers += [(((z + d) % NZ) * NG + q, y) for d in range(1, NZ)]
    for peer in peers:
        pl.semaphore_signal(barrier, inc=1, device_id=peer, device_id_type=MESH)
    pl.semaphore_wait(barrier, len(peers))

    half = rows // 2

    def gblock(c, t):
        t = (t + NY) % NY
        return gg.at[pl.ds(c * half, half), pl.ds(pl.multiple_of(t * width, width), width)]

    def gstep(c, d):
        out = []
        own = grad_ref.at[pl.ds(c * half, half)]
        if d < 4 or c == 0:
            block = gblock(c, y - d + 1)
            out.append(push(own if d == 1 else block, block, i, yr))
        if d < 4 or c == 1:
            block = gblock(c, y + d - 1)
            out.append(push(own if d == 1 else block, block, i, yl))
        return out

    def arrived(cs):
        for c in cs:
            c.wait_recv()

    def ablock(c, zz, many=2):
        return wt.at[(zz + NZ) % NZ, pl.ds(2 * c, many), core, pl.ds(0, 32), :]

    def bpiece(zz, lo=32, many=32):
        return wt.at[(zz + NZ) % NZ, x, core, pl.ds(lo, many), :]

    def bcolumn(xx, lo=0, many=NZ):
        return wt.at[pl.ds(lo, many), (xx + NX) % NX, core, pl.ds(32, 32), :]

    def same(block, dest):
        return push(block, block, dest, y)

    def astep(c, d):
        out = []
        if d < 4 or c == 0:
            out.append(same(ablock(c, z - d + 1), zr))
        if d < 4 or c == 1:
            out.append(same(ablock(c, z + d - 1), zl))
        return out

    def bstep(d):
        many = 32 if d < 4 else 16
        return [same(bpiece(z - d + 1, 32, many), zr), same(bpiece(z + d - 1, 64 - many, many), zl)]

    def xstep(h):
        block = bcolumn(x, h * NZ // 2, NZ // 2)
        return [same(block, xr), same(block, xl)]

    flight = {"X": []}
    mates = []
    flight["g01"] = gstep(0, 1)
    get_weight.wait()
    flight["b1"] = bstep(1)
    own = wt.at[z, x, core, pl.ds(0, 32), :]
    flight["a0"] = [same(own, at(z, x + d, core)) for d in range(1, NX)]
    flight["g11"] = gstep(1, 1)

    get_streams.wait()

    def widen(cg, _):
        lanes = pl.ds(pl.multiple_of(cg * LANES, LANES), LANES)
        for s in range(3):
            u32[s, cg, 8 : 8 + rows, :] = sv[s, :, lanes].astype(jnp.float32)
            tail[s, cg] = u32[s, cg, pl.ds(jnp.clip(count, 8, rows), 8), :]
        return 0

    lax.fori_loop(0, groups, widen, 0)
    tails = push(tail, halo, up, y)

    def forward(cg, _):
        lanes = pl.ds(pl.multiple_of(cg * LANES, LANES), LANES)
        coef = []
        for s in range(3):
            u32[s, cg, 0:8, :] = jnp.where(i > 0, halo[s, cg], 0.0)
            du32[s, cg, 0:TILE, :] = jnp.zeros((TILE, LANES), jnp.float32)
            du32[s, cg, TILE + rows :, :] = jnp.zeros((TILE, LANES), jnp.float32)
            dc32[s, cg, rows:, :] = jnp.zeros((8, LANES), jnp.float32)
            zbuf[s, cg] = jnp.zeros((2 * CH + 8, LANES), jnp.float32)
            for k in range(taps, 8):
                fsc[cg, s, k : k + 1, :] = jnp.zeros((1, LANES), jnp.float32)
            coef.append([fv[s, pl.ds(j, 1), lanes] for j in range(taps)])

        def chunk(r, _):
            r0 = pl.multiple_of(r * CH, CH)
            c = []
            for s in range(3):
                acc = coef[s][0] * u32[s, cg, pl.ds(8 + r0, CH), :]
                for j in range(1, taps):
                    acc = acc + coef[s][j] * u32[s, cg, pl.ds(8 + r0 - j, CH), :]
                c.append(acc)
            prod[0, cg, pl.ds(r0, CH), :] = c[1] * c[2]
            prod[1, cg, pl.ds(r0, CH), :] = c[0] * c[2]
            prod[2, cg, pl.ds(r0, CH), :] = c[0] * c[1]
            return 0

        lax.fori_loop(0, rows // CH, chunk, 0)
        return 0

    def project(b, slot):
        cols = pl.ds(pl.multiple_of(b * 256, 256), 256)
        w = wt[:, :, :, :, cols].reshape(NZ * NG * 64, 256)
        dy = jnp.dot(gg[...], w, preferred_element_type=jnp.float32)
        dyb[slot] = dy.astype(jnp.bfloat16).astype(jnp.float32)

    def gate(b, slot):
        for r in range(0, rows, CH):
            live = lax.broadcasted_iota(jnp.int32, (CH, LANES), 0) + r < count
            for e in range(2):
                dy = dyb[slot, r : r + CH, e * LANES : (e + 1) * LANES]
                for s in range(3):
                    dc = jnp.where(live, dy * prod[s, 2 * b + e, r : r + CH, :], 0.0)
                    dc32[s, 2 * b + e, r : r + CH, :] = dc.astype(jnp.bfloat16).astype(jnp.float32)
        for e in range(2):
            cg = 2 * b + e
            for s in range(3):
                acc = [jnp.zeros((8, LANES), jnp.float32)] * taps
                head[s, cg] = dc32[s, cg, 0:8, :]
                for r in range(0, rows, CH):
                    dc = dc32[s, cg, r : r + CH, :]
                    for j in range(taps):
                        term = dc * u32[s, cg, 8 + r - j : 8 + r - j + CH, :]
                        acc[j] = acc[j] + term.reshape(CH // 8, 8, LANES).sum(0)
                for j in range(taps):
                    fsc[cg, s, j : j + 1, :] = acc[j].sum(0, keepdims=True)

    def rows_back(cg, lo, hi):
        lanes = pl.ds(pl.multiple_of(cg * LANES, LANES), LANES)
        coef = [[fv[s, pl.ds(j, 1), lanes] for j in range(taps)] for s in range(3)]
        for r in range(lo, hi, CH):
            live = lax.broadcasted_iota(jnp.int32, (CH, LANES), 0) + r < count
            for s in range(3):
                acc = coef[s][0] * dc32[s, cg, r : r + CH, :]
                for j in range(1, taps):
                    acc = acc + coef[s][j] * dc32[s, cg, r + j : r + j + CH, :]
                du32[s, cg, TILE + r : TILE + r + CH, :] = jnp.where(live, acc, 0.0)

    done = 0
    for token in ORDER:
        kind = token[0]
        if kind == "f":
            if done == 0:
                get_filters.wait()
                tails.wait_recv()
            lax.fori_loop(done, done + groups // 4, forward, 0)
            done += groups // 4
            continue
        arrived(flight[token])
        if kind == "g" or kind == "A":
            c, d = int(token[1]), int(token[2])
            if d < 4:
                flight[f"{kind}{c}{d + 1}"] = (gstep if kind == "g" else astep)(c, d + 1)
            if kind == "A" and c == 1:
                mates.append(same(ablock(0, z - d, NX), mate))
                if d < 4:
                    mates.append(same(ablock(0, z + d, NX), mate))
        elif kind == "a":
            mates.append(same(ablock(0, z, NX), mate))
        elif kind == "b":
            d = int(token[1])
            if d < 4:
                flight[f"b{d + 1}"] = bstep(d + 1)
            if d == 3:
                flight["A01"], flight["A11"] = astep(0, 1), astep(1, 1)
            if d == 4:
                flight["x0"], flight["x1"] = xstep(0), xstep(1)
                mates.append(same(bcolumn(x), mate))
        elif token == "x0":
            flight["X"].append(same(bcolumn(x - 1, 0, NZ // 2), xr))
        elif token == "x1":
            flight["X"].append(same(bcolumn(x + 1, NZ // 2, NZ // 2), xl))
            mates += [same(bcolumn(x - 1), mate), same(bcolumn(x + 1), mate)]
        else:
            mates.append(same(bcolumn(x + 2), mate))
            sent = len(copies) - 3
            for c in copies[:sent]:
                c.wait_send()
    get_grad.wait()
    arrived(mates)
    arrived(flight["g04"])
    arrived(flight["g14"])

    blocks = groups // 2

    def both(b, _):
        gate(jnp.maximum(b - 1, 0), (b + 1) % 2)
        project(jnp.minimum(b, blocks - 1), b % 2)
        return 0

    lax.fori_loop(0, blocks + 1, both, 0)
    heads = push(head, heads_in, down, y)
    f1 = []
    for d in range(1, NG):
        to = (q + d) % NG
        f1.append(push(fsc.at[to], p1.at[d], z * NG + to, y))

    heads.wait_recv()

    def backward(cg, _):
        for s in range(3):
            zbuf[s, cg, CH : CH + 8, :] = jnp.where(i < n_ctx - 1, heads_in[s, cg], 0.0)

        for r in range(half, rows + 8, CH):
            size = min(CH, rows + 8 - r)
            row = jnp.clip(r - count, -CH, 8) + CH
            for s in range(3):
                dc32[s, cg, r : r + size, :] += zbuf[s, cg, pl.ds(row, size), :]
        rows_back(cg, 0, rows)

        for s in range(3):
            for k in range(SLOTS):
                block = jnp.abs(du32[s, cg, pl.ds((k + 1) * TILE - offset, TILE), :])
                top = block.reshape(TILE // 8, 8, LANES).max(0).max(0, keepdims=True)
                msc[k, pl.ds(s * groups + cg, 1), :] = top
        return 0

    lax.fori_loop(0, groups // 2, backward, 0)
    arrived(f1)
    part = fsc[q]
    for d in range(1, NG):
        part = part + p1[d]
    p2[z] = part
    f2 = []
    for d in range(1, NZ):
        f2.append(push(p2.at[z], p2.at[z], ((z + d) % NZ) * NG + q, y))
    lax.fori_loop(groups // 2, groups, backward, 0)
    tmx[...] = msc[last_slot]
    to_next = push(tmx, max_prev, up, y)
    to_prev = push(msc.at[0], max_next, down, y)

    arrived(f2)
    total = p2[0]
    for d in range(1, NZ):
        total = total + p2[d]
    fgrad_ref[q] = total
    f3 = []
    for d in range(1, NG):
        f3.append(push(fgrad_ref.at[q], fgrad_ref.at[q], z * NG + (q + d) % NG, y))

    to_next.wait_recv()
    to_prev.wait_recv()
    prev = jnp.where(offset != 0, max_prev[...], 0.0)
    follow = jnp.where((first + count) % TILE != 0, max_next[...], 0.0)
    for k in range(SLOTS):
        top = msc[k]
        if k == 0:
            top = jnp.maximum(top, prev)
        top = jnp.maximum(top, jnp.where(last_slot == k, follow, 0.0))
        scale = top + 1e-6
        inv_ref[k] = 1.0 / scale
        scales_ref[k] = jnp.where(last_slot >= k, scale, 0.0)

    arrived(f3)
    for c in copies[sent:]:
        c.wait_send()


def finish(starts_ref, du_ref, inv_ref, scale_ref, fgrad_ref, pay_out, scales_out, fgrad_out):
    s = pl.program_id(0)
    groups, rows = du_ref.shape[1], pay_out.shape[1]
    offset = starts_ref[0] % TILE
    taps = fgrad_out.shape[1]

    def group(cg, _):
        lanes = pl.ds(pl.multiple_of(cg * LANES, LANES), LANES)
        row = pl.ds(s * groups + cg, 1)
        inv = [inv_ref[k, row, :] for k in range(SLOTS)]
        for k in range(SLOTS):
            scales_out[0, k : k + 1, lanes] = scale_ref[k, row, :]
        fgrad_out[0, :, lanes] = fgrad_ref[cg, s, :taps, :]
        for r in range(0, rows, CH):
            pos = lax.broadcasted_iota(jnp.int32, (CH, LANES), 0) + (r + offset)
            scale = jnp.where(pos >= 3 * TILE, inv[3], inv[2])
            scale = jnp.where(pos >= 2 * TILE, scale, inv[1])
            scale = jnp.where(pos >= TILE, scale, inv[0])
            du = du_ref[s, cg, TILE + r : TILE + r + CH, :]
            pay_out[0, r : r + CH, lanes] = (du * scale).astype(jnp.bfloat16)
        return 0

    lax.fori_loop(0, groups, group, 0)


def shards(streams, filters, out_weight, grad_out, counts, starts):
    _, rows, channels = streams.shape
    taps = filters.shape[1]
    width = grad_out.shape[1]
    g = channels // LANES
    vmem = pl.BlockSpec(memory_space=pltpu.VMEM)
    smem = pl.BlockSpec(memory_space=pltpu.SMEM)
    hbm = pl.BlockSpec(memory_space=pltpu.HBM)
    f32, bf16 = jnp.float32, jnp.bfloat16
    V = pltpu.VMEM
    du, inv, scale, fgrad = pl.pallas_call(
        kernel,
        out_shape=(
            V((3, g, rows + 2 * TILE, LANES), f32),
            V((SLOTS, 3 * g, LANES), f32),
            V((SLOTS, 3 * g, LANES), f32),
            V((NG, 3, 8, LANES), f32),
        ),
        in_specs=[hbm, hbm, hbm, hbm, smem, smem],
        out_specs=(vmem, vmem, vmem, vmem),
        scratch_shapes=[
            V((3, rows, channels), bf16),
            V((3, taps, channels), f32),
            V((3, g, rows + 8, LANES), f32),
            V((3, g, rows, LANES), f32),
            V((NZ, NX, NC, 64, channels), bf16),
            V((rows, NY * width), bf16),
            V((2, rows, 256), f32),
            V((3, g, rows + 8, LANES), f32),
            V((3, g, 8, LANES), f32),
            V((3, g, 8, LANES), f32),
            V((3, g, 8, LANES), f32),
            V((3, g, 8, LANES), f32),
            V((3, g, 2 * CH + 8, LANES), f32),
            V((SLOTS, 3 * g, LANES), f32),
            V((3 * g, LANES), f32),
            V((3 * g, LANES), f32),
            V((3 * g, LANES), f32),
            V((g, 3, 8, LANES), f32),
            V((NG, 3, 8, LANES), f32),
            V((NZ, 3, 8, LANES), f32),
            pltpu.SemaphoreType.DMA((96,)),
            pltpu.SemaphoreType.DMA((96,)),
            pltpu.SemaphoreType.DMA((4,)),
        ],
        compiler_params=pltpu.CompilerParams(
            collective_id=0, has_side_effects=True, vmem_limit_bytes=VLIM * 1024 * 1024
        ),
        cost_estimate=pl.CostEstimate(
            flops=2 * rows * channels * NY * width, bytes_accessed=12 * rows * channels, transcendentals=0
        ),
    )(streams, filters, out_weight.T, grad_out, counts, starts)
    return pl.pallas_call(
        finish,
        grid=(3,),
        out_shape=(
            jax.ShapeDtypeStruct((3, rows, channels), bf16),
            jax.ShapeDtypeStruct((3, SLOTS, channels), f32),
            jax.ShapeDtypeStruct((3, taps, channels), f32),
        ),
        in_specs=[smem, vmem, vmem, vmem, vmem],
        out_specs=(
            pl.BlockSpec((1, rows, channels), lambda s: (s, 0, 0)),
            pl.BlockSpec((1, SLOTS, channels), lambda s: (s, 0, 0)),
            pl.BlockSpec((1, taps, channels), lambda s: (s, 0, 0)),
        ),
        compiler_params=pltpu.CompilerParams(vmem_limit_bytes=20 * 1024 * 1024),
    )(starts, du, inv, scale, fgrad)


def solution(mesh):
    return jax.shard_map(
        shards,
        mesh=mesh,
        in_specs=(
            P(None, "ctx", "tp"),
            P(None, None, "tp"),
            P("tp", "ctx"),
            P("ctx", "tp"),
            P("ctx"),
            P("ctx"),
        ),
        out_specs=(P(None, "ctx", "tp"), P(None, "ctx", "tp"), P(None, None, "tp")),
        check_vma=False,
    )
```

```python
import functools

import jax
import jax.numpy as jnp
from jax import lax
from jax.experimental import pallas as pl
from jax.experimental.pallas import tpu as pltpu
from jax.sharding import PartitionSpec as P

MESH = pl.DeviceIdType.MESH
TILE = 128
LANES = 128
NZ, NX, NC, NY = 8, 4, 2, 8
NG = NX * NC
CH = 64
SLOTS = 4
VLIM = 54


ORDER = (
    "b1", "m", "b2", "a0", "g01", "b3", "b4", "f", "f", "g11", "f", "f", "A01", "g02", "A11", "x0",
    "A02", "g12", "A12", "x1", "g03", "A03", "A13", "g13", "X", "A04", "A14",
)


def kernel(
    streams_ref, filters_ref, weight_ref, grad_ref, counts_ref, starts_ref,
    du32, inv_ref, scales_ref, fgrad_ref,
    sv, fv, gv, give, u32, prod, wt, gg, own_dy, part_out, part_in, dc32, tail, halo, head, heads_in, zbuf,
    msc, tmx, max_prev, max_next, fsc, p1, p2,
    send, recv, psend, precv, local,
):
    rows = grad_ref.shape[0]
    width = grad_ref.shape[1]
    taps = filters_ref.shape[1]
    groups = weight_ref.shape[1] // LANES
    i = lax.axis_index("ctx")
    y = lax.axis_index("tp")
    z = i // NG
    q = i % NG
    x = q // NC
    core = q % NC
    n_ctx = NZ * NG

    count = counts_ref[0]
    first = starts_ref[0]
    offset = first % TILE
    last_slot = jnp.clip((offset + count - 1) // TILE, 0, SLOTS - 1)

    def at(zz, xx, cc):
        return ((zz + NZ) % NZ) * NG + ((xx + NX) % NX) * NC + cc

    copies = []

    def push(src, dst, ctx, tp):
        k = len(copies)
        c = pltpu.make_async_remote_copy(
            src_ref=src, dst_ref=dst, send_sem=send.at[k], recv_sem=recv.at[k],
            device_id=(ctx, tp), device_id_type=MESH,
        )
        c.start()
        copies.append(c)
        return c

    up, down = (i + 1) % n_ctx, (i + n_ctx - 1) % n_ctx
    yr, yl = (y + 1) % NY, (y + NY - 1) % NY
    zr, zl = at(z + 1, x, core), at(z - 1, x, core)
    xr, xl = at(z, x + 1, core), at(z, x - 1, core)
    mate = at(z, x, 1 - core)

    get_streams = pltpu.make_async_copy(streams_ref, sv, local.at[0])
    get_streams.start()
    get_grad = pltpu.make_async_copy(grad_ref, gv, local.at[1])
    get_grad.start()

    get_weight = pltpu.make_async_copy(weight_ref, wt.at[z, x], local.at[2])
    get_weight.start()
    get_filters = pltpu.make_async_copy(filters_ref, fv, local.at[3])
    get_filters.start()

    barrier = pltpu.get_barrier_semaphore()
    peers = [(i, yr), (i, yl), (up, y), (down, y)]
    peers += [(z * NG + (q + d) % NG, y) for d in range(1, NG)]
    peers += [(((z + d) % NZ) * NG + q, y) for d in range(1, NZ)]
    for peer in peers:
        pl.semaphore_signal(barrier, inc=1, device_id=peer, device_id_type=MESH)

    half = rows // 2
    keep = width // 2
    mine = pl.ds(pl.multiple_of(y * keep, keep), keep)
    get_grad.wait()

    def sort_columns(r, _):
        r0 = pl.multiple_of(r * CH, CH)
        v = gv[pl.ds(r0, CH), :].astype(jnp.float32)
        piece = [v[:, 64 * e : 64 * (e + 1)] for e in range(NG)]
        even = jnp.concatenate(piece[0::2], axis=1)
        odd = jnp.concatenate(piece[1::2], axis=1)
        gg[pl.ds(r0, CH), mine] = jnp.where(core == 0, even, odd).astype(jnp.bfloat16)
        give[pl.ds(r0, CH), :] = jnp.where(core == 0, odd, even).astype(jnp.bfloat16)
        return 0

    lax.fori_loop(0, rows // CH, sort_columns, 0)
    pl.semaphore_wait(barrier, len(peers))

    def gblock(c, t):
        t = (t + NY) % NY
        return gg.at[pl.ds(c * rows, rows), pl.ds(pl.multiple_of(t * keep, keep), keep)]

    def gstep(c, d):
        out = []
        if d < 4 or c == 0:
            block = gblock(c, y - d + 1)
            out.append(push(block, block, i, yr))
        if d < 4 or c == 1:
            block = gblock(c, y + d - 1)
            out.append(push(block, block, i, yl))
        return out

    def arrived(cs):
        for c in cs:
            c.wait_recv()

    def ablock(c, zz, many=2):
        return wt.at[(zz + NZ) % NZ, pl.ds(2 * c, many), pl.ds(0, 32), :]

    def bpiece(zz, lo=32, many=32):
        return wt.at[(zz + NZ) % NZ, x, pl.ds(lo, many), :]

    def bcolumn(xx, lo=0, many=NZ):
        return wt.at[pl.ds(lo, many), (xx + NX) % NX, pl.ds(32, 32), :]

    def same(block, dest):
        return push(block, block, dest, y)

    def astep(c, d):
        out = []
        if d < 4 or c == 0:
            out.append(same(ablock(c, z - d + 1), zr))
        if d < 4 or c == 1:
            out.append(same(ablock(c, z + d - 1), zl))
        return out

    def bstep(d):
        many = 32 if d < 4 else 16
        return [same(bpiece(z - d + 1, 32, many), zr), same(bpiece(z + d - 1, 64 - many, many), zl)]

    def xstep(h):
        block = bcolumn(x, h * NZ // 2, NZ // 2)
        return [same(block, xr), same(block, xl)]

    flight = {"X": []}
    flight["m"] = [push(give, gg.at[pl.ds(rows, rows), mine], mate, y)]
    flight["g01"] = gstep(0, 1)
    get_weight.wait()
    flight["b1"] = bstep(1)
    own = wt.at[z, x, pl.ds(0, 32), :]
    flight["a0"] = [same(own, at(z, x + d, core)) for d in range(1, NX)]

    get_streams.wait()

    def widen(cg, _):
        lanes = pl.ds(pl.multiple_of(cg * LANES, LANES), LANES)
        for s in range(3):
            u32[s, cg, 8 : 8 + rows, :] = sv[s, :, lanes].astype(jnp.float32)
            tail[s, cg] = u32[s, cg, pl.ds(jnp.clip(count, 8, rows), 8), :]
        return 0

    lax.fori_loop(0, groups, widen, 0)
    tails = push(tail, halo, up, y)

    def forward(cg, _):
        lanes = pl.ds(pl.multiple_of(cg * LANES, LANES), LANES)
        coef = []
        for s in range(3):
            u32[s, cg, 0:8, :] = jnp.where(i > 0, halo[s, cg], 0.0)
            du32[s, cg, 0:TILE, :] = jnp.zeros((TILE, LANES), jnp.float32)
            du32[s, cg, TILE + rows :, :] = jnp.zeros((TILE, LANES), jnp.float32)
            dc32[s, cg, rows:, :] = jnp.zeros((8, LANES), jnp.float32)
            zbuf[s, cg] = jnp.zeros((2 * CH + 8, LANES), jnp.float32)
            for k in range(taps, 8):
                fsc[cg, s, k : k + 1, :] = jnp.zeros((1, LANES), jnp.float32)
            coef.append([fv[s, pl.ds(j, 1), lanes] for j in range(taps)])

        def chunk(r, _):
            r0 = pl.multiple_of(r * CH, CH)
            c = []
            for s in range(3):
                acc = coef[s][0] * u32[s, cg, pl.ds(8 + r0, CH), :]
                for j in range(1, taps):
                    acc = acc + coef[s][j] * u32[s, cg, pl.ds(8 + r0 - j, CH), :]
                c.append(acc)
            prod[0, cg, pl.ds(r0, CH), :] = c[1] * c[2]
            prod[1, cg, pl.ds(r0, CH), :] = c[0] * c[2]
            prod[2, cg, pl.ds(r0, CH), :] = c[0] * c[1]
            return 0

        lax.fori_loop(0, rows // CH, chunk, 0)
        return 0

    def project(b, slot):
        cols = pl.ds(pl.multiple_of(jnp.minimum(b, blocks - 1) * 256, 256), 256)
        w = wt[:, :, :, cols].reshape(NZ * NX * 64, 256)
        theirs = jnp.dot(gg[rows:, :], w, preferred_element_type=jnp.float32)
        part_out[b] = theirs.astype(jnp.bfloat16)
        own_dy[slot] = jnp.dot(gg[:rows, :], w, preferred_element_type=jnp.float32)

    def partial(b):
        return pltpu.make_async_remote_copy(
            src_ref=part_out.at[b], dst_ref=part_in.at[b], send_sem=psend.at[b], recv_sem=precv.at[b],
            device_id=(mate, y), device_id_type=MESH,
        )

    def gate(b, slot, got):
        for r in range(0, rows, CH):
            live = lax.broadcasted_iota(jnp.int32, (CH, LANES), 0) + r < count
            for e in range(2):
                lanes = slice(e * LANES, (e + 1) * LANES)
                dy = own_dy[slot, r : r + CH, lanes] + part_in[got, r : r + CH, lanes].astype(jnp.float32)
                dy = dy.astype(jnp.bfloat16).astype(jnp.float32)
                for s in range(3):
                    dc = jnp.where(live, dy * prod[s, 2 * b + e, r : r + CH, :], 0.0)
                    dc32[s, 2 * b + e, r : r + CH, :] = dc.astype(jnp.bfloat16).astype(jnp.float32)
        for e in range(2):
            cg = 2 * b + e
            for s in range(3):
                acc = [jnp.zeros((8, LANES), jnp.float32)] * taps
                head[s, cg] = dc32[s, cg, 0:8, :]
                for r in range(0, rows, CH):
                    dc = dc32[s, cg, r : r + CH, :]
                    for j in range(taps):
                        term = dc * u32[s, cg, 8 + r - j : 8 + r - j + CH, :]
                        acc[j] = acc[j] + term.reshape(CH // 8, 8, LANES).sum(0)
                for j in range(taps):
                    fsc[cg, s, j : j + 1, :] = acc[j].sum(0, keepdims=True)

    def rows_back(cg, lo, hi):
        lanes = pl.ds(pl.multiple_of(cg * LANES, LANES), LANES)
        coef = [[fv[s, pl.ds(j, 1), lanes] for j in range(taps)] for s in range(3)]
        for r in range(lo, hi, CH):
            live = lax.broadcasted_iota(jnp.int32, (CH, LANES), 0) + r < count
            for s in range(3):
                acc = coef[s][0] * dc32[s, cg, r : r + CH, :]
                for j in range(1, taps):
                    acc = acc + coef[s][j] * dc32[s, cg, r + j : r + j + CH, :]
                du32[s, cg, TILE + r : TILE + r + CH, :] = jnp.where(live, acc, 0.0)

    blocks = groups // 2
    done = 0
    for token in ORDER:
        kind = token[0]
        if kind == "f":
            if done == 0:
                get_filters.wait()
                tails.wait_recv()
            lax.fori_loop(done, done + groups // 4, forward, 0)
            done += groups // 4
            continue
        arrived(flight[token])
        if kind == "g" or kind == "A":
            c, d = int(token[1]), int(token[2])
            if d < 4:
                flight[f"{kind}{c}{d + 1}"] = (gstep if kind == "g" else astep)(c, d + 1)
        elif kind == "m":
            flight["g11"] = gstep(1, 1)
        elif kind == "b":
            d = int(token[1])
            if d < 4:
                flight[f"b{d + 1}"] = bstep(d + 1)
            if d == 3:
                flight["A01"], flight["A11"] = astep(0, 1), astep(1, 1)
            if d == 4:
                flight["x0"], flight["x1"] = xstep(0), xstep(1)
        elif token == "x0":
            flight["X"].append(same(bcolumn(x - 1, 0, NZ // 2), xr))
        elif token == "x1":
            flight["X"].append(same(bcolumn(x + 1, NZ // 2, NZ // 2), xl))
        elif token == "X":
            sent = len(copies) - 2
            for c in copies[:sent]:
                c.wait_send()
    arrived(flight["g04"])
    arrived(flight["g14"])

    def both(b, _):
        @pl.when(b >= 1)
        def _():
            partial(b - 1).wait_recv()

        gate(jnp.maximum(b - 1, 0), (b + 1) % 2, (b + blocks) % (blocks + 1))
        project(b, b % 2)

        @pl.when(b < blocks)
        def _():
            partial(b).start()

        return 0

    lax.fori_loop(0, blocks + 1, both, 0)
    heads = push(head, heads_in, down, y)
    f1 = []
    for d in range(1, NG):
        to = (q + d) % NG
        f1.append(push(fsc.at[to], p1.at[d], z * NG + to, y))

    heads.wait_recv()

    def backward(cg, _):
        for s in range(3):
            zbuf[s, cg, CH : CH + 8, :] = jnp.where(i < n_ctx - 1, heads_in[s, cg], 0.0)

        for r in range(half, rows + 8, CH):
            size = min(CH, rows + 8 - r)
            row = jnp.clip(r - count, -CH, 8) + CH
            for s in range(3):
                dc32[s, cg, r : r + size, :] += zbuf[s, cg, pl.ds(row, size), :]
        rows_back(cg, 0, rows)

        for s in range(3):
            for k in range(SLOTS):
                block = jnp.abs(du32[s, cg, pl.ds((k + 1) * TILE - offset, TILE), :])
                top = block.reshape(TILE // 8, 8, LANES).max(0).max(0, keepdims=True)
                msc[k, pl.ds(s * groups + cg, 1), :] = top
        return 0

    lax.fori_loop(0, groups // 2, backward, 0)
    arrived(f1)
    part = fsc[q]
    for d in range(1, NG):
        part = part + p1[d]
    p2[z] = part
    f2 = []
    for d in range(1, NZ):
        f2.append(push(p2.at[z], p2.at[z], ((z + d) % NZ) * NG + q, y))
    lax.fori_loop(groups // 2, groups, backward, 0)
    tmx[...] = msc[last_slot]
    to_next = push(tmx, max_prev, up, y)
    to_prev = push(msc.at[0], max_next, down, y)

    arrived(f2)
    total = p2[0]
    for d in range(1, NZ):
        total = total + p2[d]
    fgrad_ref[q] = total
    f3 = []
    for d in range(1, NG):
        f3.append(push(fgrad_ref.at[q], fgrad_ref.at[q], z * NG + (q + d) % NG, y))

    to_next.wait_recv()
    to_prev.wait_recv()
    prev = jnp.where(offset != 0, max_prev[...], 0.0)
    follow = jnp.where((first + count) % TILE != 0, max_next[...], 0.0)
    for k in range(SLOTS):
        top = msc[k]
        if k == 0:
            top = jnp.maximum(top, prev)
        top = jnp.maximum(top, jnp.where(last_slot == k, follow, 0.0))
        scale = top + 1e-6
        inv_ref[k] = 1.0 / scale
        scales_ref[k] = jnp.where(last_slot >= k, scale, 0.0)

    arrived(f3)
    for c in copies[sent:]:
        c.wait_send()
    for b in range(blocks):
        partial(b).wait_send()


def finish(starts_ref, du_ref, inv_ref, scale_ref, fgrad_ref, pay_out, scales_out, fgrad_out):
    s = pl.program_id(0)
    groups, rows = du_ref.shape[1], pay_out.shape[1]
    offset = starts_ref[0] % TILE
    taps = fgrad_out.shape[1]

    def group(cg, _):
        lanes = pl.ds(pl.multiple_of(cg * LANES, LANES), LANES)
        row = pl.ds(s * groups + cg, 1)
        inv = [inv_ref[k, row, :] for k in range(SLOTS)]
        for k in range(SLOTS):
            scales_out[0, k : k + 1, lanes] = scale_ref[k, row, :]
        fgrad_out[0, :, lanes] = fgrad_ref[cg, s, :taps, :]
        for r in range(0, rows, CH):
            pos = lax.broadcasted_iota(jnp.int32, (CH, LANES), 0) + (r + offset)
            scale = jnp.where(pos >= 3 * TILE, inv[3], inv[2])
            scale = jnp.where(pos >= 2 * TILE, scale, inv[1])
            scale = jnp.where(pos >= TILE, scale, inv[0])
            du = du_ref[s, cg, TILE + r : TILE + r + CH, :]
            pay_out[0, r : r + CH, lanes] = (du * scale).astype(jnp.bfloat16)
        return 0

    lax.fori_loop(0, groups, group, 0)


def shards(streams, filters, out_weight, grad_out, counts, starts):
    _, rows, channels = streams.shape
    taps = filters.shape[1]
    width = grad_out.shape[1]
    g = channels // LANES
    vmem = pl.BlockSpec(memory_space=pltpu.VMEM)
    smem = pl.BlockSpec(memory_space=pltpu.SMEM)
    hbm = pl.BlockSpec(memory_space=pltpu.HBM)
    f32, bf16 = jnp.float32, jnp.bfloat16
    V = pltpu.VMEM
    du, inv, scale, fgrad = pl.pallas_call(
        kernel,
        out_shape=(
            V((3, g, rows + 2 * TILE, LANES), f32),
            V((SLOTS, 3 * g, LANES), f32),
            V((SLOTS, 3 * g, LANES), f32),
            V((NG, 3, 8, LANES), f32),
        ),
        in_specs=[hbm, hbm, hbm, hbm, smem, smem],
        out_specs=(vmem, vmem, vmem, vmem),
        scratch_shapes=[
            V((3, rows, channels), bf16),
            V((3, taps, channels), f32),
            V((rows, width), bf16),
            V((rows, width // 2), bf16),
            V((3, g, rows + 8, LANES), f32),
            V((3, g, rows, LANES), f32),
            V((NZ, NX, 64, channels), bf16),
            V((2 * rows, NY * width // 2), bf16),
            V((2, rows, 256), f32),
            V((g // 2 + 1, rows, 256), bf16),
            V((g // 2 + 1, rows, 256), bf16),
            V((3, g, rows + 8, LANES), f32),
            V((3, g, 8, LANES), f32),
            V((3, g, 8, LANES), f32),
            V((3, g, 8, LANES), f32),
            V((3, g, 8, LANES), f32),
            V((3, g, 2 * CH + 8, LANES), f32),
            V((SLOTS, 3 * g, LANES), f32),
            V((3 * g, LANES), f32),
            V((3 * g, LANES), f32),
            V((3 * g, LANES), f32),
            V((g, 3, 8, LANES), f32),
            V((NG, 3, 8, LANES), f32),
            V((NZ, 3, 8, LANES), f32),
            pltpu.SemaphoreType.DMA((96,)),
            pltpu.SemaphoreType.DMA((96,)),
            pltpu.SemaphoreType.DMA((g // 2,)),
            pltpu.SemaphoreType.DMA((g // 2,)),
            pltpu.SemaphoreType.DMA((4,)),
        ],
        compiler_params=pltpu.CompilerParams(
            collective_id=0, has_side_effects=True, vmem_limit_bytes=VLIM * 1024 * 1024
        ),
        cost_estimate=pl.CostEstimate(
            flops=2 * rows * channels * NY * width, bytes_accessed=12 * rows * channels, transcendentals=0
        ),
    )(streams, filters, out_weight.T, grad_out, counts, starts)
    return pl.pallas_call(
        finish,
        grid=(3,),
        out_shape=(
            jax.ShapeDtypeStruct((3, rows, channels), bf16),
            jax.ShapeDtypeStruct((3, SLOTS, channels), f32),
            jax.ShapeDtypeStruct((3, taps, channels), f32),
        ),
        in_specs=[smem, vmem, vmem, vmem, vmem],
        out_specs=(
            pl.BlockSpec((1, rows, channels), lambda s: (s, 0, 0)),
            pl.BlockSpec((1, SLOTS, channels), lambda s: (s, 0, 0)),
            pl.BlockSpec((1, taps, channels), lambda s: (s, 0, 0)),
        ),
        compiler_params=pltpu.CompilerParams(vmem_limit_bytes=20 * 1024 * 1024),
    )(starts, du, inv, scale, fgrad)


def solution(mesh):
    return jax.shard_map(
        shards,
        mesh=mesh,
        in_specs=(
            P(None, "ctx", "tp"),
            P(None, None, "tp"),
            P("tp", "ctx"),
            P("ctx", "tp"),
            P("ctx"),
            P("ctx"),
        ),
        out_specs=(P(None, "ctx", "tp"), P(None, "ctx", "tp"), P(None, None, "tp")),
        check_vma=False,
    )
```

```python
import functools

import jax
import jax.numpy as jnp
from jax import lax
from jax.experimental import pallas as pl
from jax.experimental.pallas import tpu as pltpu
from jax.sharding import PartitionSpec as P

MESH = pl.DeviceIdType.MESH
TILE = 128
LANES = 128
NZ, NX, NC, NY = 8, 4, 2, 8
NG = NX * NC
CH = 64
SLOTS = 4
STEP = 49
VLIM = 54


ORDER = (
    "b1", "b2", "g01", "a0", "b3", "b4", "f", "g11", "f", "f", "A01", "f", "g02", "A11", "x0",
    "A02", "g12", "A12", "x1", "g03", "A03", "A13", "g13", "X", "A04", "A14",
)


def kernel(
    streams_ref, filters_ref, weight_ref, grad_ref, counts_ref, starts_ref,
    du32, inv_ref, scales_ref, fgrad_ref,
    sv, fv, u32, prod, wt, gg, dyb, dc32, tail, halo, head, heads_in, zbuf,
    msc, tmx, max_prev, max_next, fsc, p1, p2,
    send, recv, local,
):
    rows = grad_ref.shape[0]
    width = grad_ref.shape[1]
    taps = filters_ref.shape[1]
    groups = weight_ref.shape[1] // LANES
    i = lax.axis_index("ctx")
    y = lax.axis_index("tp")
    z = i // NG
    q = i % NG
    x = q // NC
    core = q % NC
    n_ctx = NZ * NG

    count = counts_ref[0]
    first = starts_ref[0]
    offset = first % TILE
    last_slot = jnp.clip((offset + count - 1) // TILE, 0, SLOTS - 1)

    def at(zz, xx, cc):
        return ((zz + NZ) % NZ) * NG + ((xx + NX) % NX) * NC + cc

    copies = []

    def push(src, dst, ctx, tp):
        k = len(copies)
        c = pltpu.make_async_remote_copy(
            src_ref=src, dst_ref=dst, send_sem=send.at[k], recv_sem=recv.at[k],
            device_id=(ctx, tp), device_id_type=MESH,
        )
        c.start()
        copies.append(c)
        return c

    up, down = (i + 1) % n_ctx, (i + n_ctx - 1) % n_ctx
    yr, yl = (y + 1) % NY, (y + NY - 1) % NY
    zr, zl = at(z + 1, x, core), at(z - 1, x, core)
    xr, xl = at(z, x + 1, core), at(z, x - 1, core)
    mate = at(z, x, 1 - core)

    get_streams = pltpu.make_async_copy(streams_ref, sv, local.at[0])
    get_streams.start()
    own_cols = pl.ds(pl.multiple_of(y * width, width), width)
    get_grad = pltpu.make_async_copy(grad_ref, gg.at[:, own_cols], local.at[1])
    get_grad.start()

    get_weight = pltpu.make_async_copy(weight_ref, wt.at[z, x, core], local.at[2])
    get_weight.start()
    get_filters = pltpu.make_async_copy(filters_ref, fv, local.at[3])
    get_filters.start()

    barrier = pltpu.get_barrier_semaphore()
    peers = [(i, yr), (i, yl), (up, y), (down, y)]
    peers += [(z * NG + (q + d) % NG, y) for d in range(1, NG)]
    peers += [(((z + d) % NZ) * NG + q, y) for d in range(1, NZ)]
    for peer in peers:
        pl.semaphore_signal(barrier, inc=1, device_id=peer, device_id_type=MESH)
    pl.semaphore_wait(barrier, len(peers))

    half = rows // 2

    def gblock(c, t):
        t = (t + NY) % NY
        return gg.at[pl.ds(c * half, half), pl.ds(pl.multiple_of(t * width, width), width)]

    def gstep(c, d):
        out = []
        own = grad_ref.at[pl.ds(c * half, half)]
        if d < 4 or c == 0:
            block = gblock(c, y - d + 1)
            out.append(push(own if d == 1 else block, block, i, yr))
        if d < 4 or c == 1:
            block = gblock(c, y + d - 1)
            out.append(push(own if d == 1 else block, block, i, yl))
        return out

    def arrived(cs):
        for c in cs:
            c.wait_recv()

    def ablock(c, zz, many=2):
        return wt.at[(zz + NZ) % NZ, pl.ds(2 * c, many), core, pl.ds(0, 32), :]

    def bpiece(zz, lo=32, many=32):
        return wt.at[(zz + NZ) % NZ, x, core, pl.ds(lo, many), :]

    def bcolumn(xx, lo=0, many=NZ):
        return wt.at[pl.ds(lo, many), (xx + NX) % NX, core, pl.ds(32, 32), :]

    def same(block, dest):
        return push(block, block, dest, y)

    def astep(c, d):
        out = []
        if d < 4 or c == 0:
            out.append(same(ablock(c, z - d + 1), zr))
        if d < 4 or c == 1:
            out.append(same(ablock(c, z + d - 1), zl))
        return out

    def bstep(d):
        many = 32 if d < 4 else 16
        return [same(bpiece(z - d + 1, 32, many), zr), same(bpiece(z + d - 1, 64 - many, many), zl)]

    def xstep(h):
        block = bcolumn(x, h * NZ // 2, NZ // 2)
        return [same(block, xr), same(block, xl)]

    flight = {"X": []}
    mates = []
    flight["g01"] = gstep(0, 1)
    get_weight.wait()
    flight["b1"] = bstep(1)
    own = wt.at[z, x, core, pl.ds(0, 32), :]
    flight["a0"] = [same(own, at(z, x + d, core)) for d in range(1, NX)]
    flight["g11"] = gstep(1, 1)

    get_streams.wait()

    def widen(cg, _):
        lanes = pl.ds(pl.multiple_of(cg * LANES, LANES), LANES)
        for s in range(3):
            u32[s, cg, 8 : 8 + rows, :] = sv[s, :, lanes].astype(jnp.float32)
            u32[s, cg, 8 + rows :, :] = jnp.zeros((8, LANES), jnp.float32)
            tail[s, cg] = u32[s, cg, pl.ds(jnp.clip(count, 8, rows), 8), :]
        return 0

    lax.fori_loop(0, groups, widen, 0)
    tails = push(tail, halo, up, y)

    def strided(start):
        return pl.ds(start, 8, stride=STEP)

    def tapped(f, w):
        acc = f[0] * w[0]
        for j in range(1, taps):
            acc = acc + f[j] * w[j]
        return acc

    sub = lax.broadcasted_iota(jnp.int32, (8, LANES), 0) * STEP

    def forward(cg, _):
        lanes = pl.ds(pl.multiple_of(cg * LANES, LANES), LANES)
        coef = []
        for s in range(3):
            u32[s, cg, 0:8, :] = jnp.where(i > 0, halo[s, cg], 0.0)
            dc32[s, cg, rows:, :] = jnp.zeros((16, LANES), jnp.float32)
            zbuf[s, cg] = jnp.zeros((rows + 16, LANES), jnp.float32)
            for k in range(taps, 8):
                fsc[cg, s, k : k + 1, :] = jnp.zeros((1, LANES), jnp.float32)
            coef.append([fv[s, pl.ds(j, 1), lanes] for j in range(taps)])

        spread = [[jnp.broadcast_to(f, (8, LANES)) for f in fs] for fs in coef]
        window = [[u32[s, cg, strided(8 - j), :] for j in range(1, taps)] for s in range(3)]
        for k in range(STEP):
            c = []
            for s in range(3):
                window[s] = [u32[s, cg, strided(8 + k), :]] + window[s][: taps - 1]
                c.append(tapped(spread[s], window[s]))
            prod[0, cg, k] = c[1] * c[2]
            prod[1, cg, k] = c[0] * c[2]
            prod[2, cg, k] = c[0] * c[1]
        return 0

    def project(b, slot):
        cols = pl.ds(pl.multiple_of(b * 256, 256), 256)
        w = wt[:, :, :, :, cols].reshape(NZ * NG * 64, 256)
        dy = jnp.dot(gg[...], w, preferred_element_type=jnp.float32)
        dy = dy.astype(jnp.bfloat16).astype(jnp.float32)
        dyb[slot, 0, :rows, :] = dy[:, :LANES]
        dyb[slot, 1, :rows, :] = dy[:, LANES:]

    def gate(b, slot):
        for e in range(2):
            cg = 2 * b + e
            for s in range(3):
                acc = [jnp.zeros((8, LANES), jnp.float32)] * taps
                window = [u32[s, cg, strided(8 - j), :] for j in range(1, taps)]
                for k in range(STEP):
                    window = [u32[s, cg, strided(8 + k), :]] + window[: taps - 1]
                    dc = jnp.where(sub < count - k, dyb[slot, e, strided(k), :] * prod[s, cg, k], 0.0)
                    dc = dc.astype(jnp.bfloat16).astype(jnp.float32)
                    dc32[s, cg, strided(k), :] = dc
                    acc = [acc[j] + dc * window[j] for j in range(taps)]
                for j in range(taps):
                    fsc[cg, s, j : j + 1, :] = acc[j].sum(0, keepdims=True)
                head[s, cg] = dc32[s, cg, 0:8, :]

    done = 0
    for token in ORDER:
        kind = token[0]
        if kind == "f":
            if done == 0:
                get_filters.wait()
                tails.wait_recv()
            lax.fori_loop(done, done + groups // 4, forward, 0)
            done += groups // 4
            continue
        arrived(flight[token])
        if kind == "g" or kind == "A":
            c, d = int(token[1]), int(token[2])
            if d < 4:
                flight[f"{kind}{c}{d + 1}"] = (gstep if kind == "g" else astep)(c, d + 1)
            if kind == "A" and c == 1:
                mates.append(same(ablock(0, z - d, NX), mate))
                if d < 4:
                    mates.append(same(ablock(0, z + d, NX), mate))
        elif kind == "a":
            mates.append(same(ablock(0, z, NX), mate))
        elif kind == "b":
            d = int(token[1])
            if d < 4:
                flight[f"b{d + 1}"] = bstep(d + 1)
            if d == 3:
                flight["A01"], flight["A11"] = astep(0, 1), astep(1, 1)
            if d == 4:
                flight["x0"], flight["x1"] = xstep(0), xstep(1)
                mates.append(same(bcolumn(x), mate))
        elif token == "x0":
            flight["X"].append(same(bcolumn(x - 1, 0, NZ // 2), xr))
        elif token == "x1":
            flight["X"].append(same(bcolumn(x + 1, NZ // 2, NZ // 2), xl))
            mates += [same(bcolumn(x - 1), mate), same(bcolumn(x + 1), mate)]
        else:
            mates.append(same(bcolumn(x + 2), mate))
            sent = len(copies) - 3
            for c in copies[:sent]:
                c.wait_send()
    get_grad.wait()
    arrived(mates)
    arrived(flight["g04"])
    arrived(flight["g14"])

    blocks = groups // 2

    def both(b, _):
        gate(jnp.maximum(b - 1, 0), (b + 1) % 2)
        project(jnp.minimum(b, blocks - 1), b % 2)
        return 0

    lax.fori_loop(0, blocks + 1, both, 0)
    heads = push(head, heads_in, down, y)
    f1 = []
    for d in range(1, NG):
        to = (q + d) % NG
        f1.append(push(fsc.at[to], p1.at[d], z * NG + to, y))

    heads.wait_recv()

    held = jnp.clip(count, half, rows)

    def backward(cg, _):
        lanes = pl.ds(pl.multiple_of(cg * LANES, LANES), LANES)
        for s in range(3):
            zbuf[s, cg, half : half + 8, :] = jnp.where(i < n_ctx - 1, heads_in[s, cg], 0.0)

        leap = (rows - half + 8) // 8
        for m in range(leap):
            to = pl.ds(half + m, 8, stride=leap)
            for s in range(3):
                dc32[s, cg, to, :] += zbuf[s, cg, pl.ds(rows + m - held, 8, stride=leap), :]

        low = (sub + offset) // TILE
        border = (low + 1) * TILE - offset - sub
        for s in range(3):
            f = [jnp.broadcast_to(fv[s, pl.ds(j, 1), lanes], (8, LANES)) for j in range(taps)]
            window = [dc32[s, cg, strided(j), :] for j in range(taps - 1)]
            before = jnp.zeros((8, LANES), jnp.float32)
            after = before
            for k in range(STEP):
                window = window[-(taps - 1) :] + [dc32[s, cg, strided(k + taps - 1), :]]
                du = jnp.where(sub < count - k, tapped(f, window), 0.0)
                du32[s, cg, strided(k), :] = du
                size = jnp.abs(du)
                before = jnp.maximum(before, jnp.where(border > k, size, 0.0))
                after = jnp.maximum(after, jnp.where(border > k, 0.0, size))
            for k in range(SLOTS):
                top = jnp.maximum(jnp.where(low == k, before, 0.0), jnp.where(low == k - 1, after, 0.0))
                msc[k, pl.ds(s * groups + cg, 1), :] = top.max(0, keepdims=True)
        return 0

    lax.fori_loop(0, groups // 2, backward, 0)
    arrived(f1)
    part = fsc[q]
    for d in range(1, NG):
        part = part + p1[d]
    p2[z] = part
    f2 = []
    for d in range(1, NZ):
        f2.append(push(p2.at[z], p2.at[z], ((z + d) % NZ) * NG + q, y))
    lax.fori_loop(groups // 2, groups, backward, 0)
    tmx[...] = msc[last_slot]
    to_next = push(tmx, max_prev, up, y)
    to_prev = push(msc.at[0], max_next, down, y)

    arrived(f2)
    total = p2[0]
    for d in range(1, NZ):
        total = total + p2[d]
    fgrad_ref[q] = total
    f3 = []
    for d in range(1, NG):
        f3.append(push(fgrad_ref.at[q], fgrad_ref.at[q], z * NG + (q + d) % NG, y))

    to_next.wait_recv()
    to_prev.wait_recv()
    prev = jnp.where(offset != 0, max_prev[...], 0.0)
    follow = jnp.where((first + count) % TILE != 0, max_next[...], 0.0)
    for k in range(SLOTS):
        top = msc[k]
        if k == 0:
            top = jnp.maximum(top, prev)
        top = jnp.maximum(top, jnp.where(last_slot == k, follow, 0.0))
        scale = top + 1e-6
        inv_ref[k] = 1.0 / scale
        scales_ref[k] = jnp.where(last_slot >= k, scale, 0.0)

    arrived(f3)
    for c in copies[sent:]:
        c.wait_send()


def finish(starts_ref, du_ref, inv_ref, scale_ref, fgrad_ref, pay_out, scales_out, fgrad_out):
    s = pl.program_id(0)
    groups, rows = du_ref.shape[1], pay_out.shape[1]
    offset = starts_ref[0] % TILE
    taps = fgrad_out.shape[1]

    def group(cg, _):
        lanes = pl.ds(pl.multiple_of(cg * LANES, LANES), LANES)
        row = pl.ds(s * groups + cg, 1)
        inv = [inv_ref[k, row, :] for k in range(SLOTS)]
        for k in range(SLOTS):
            scales_out[0, k : k + 1, lanes] = scale_ref[k, row, :]
        fgrad_out[0, :, lanes] = fgrad_ref[cg, s, :taps, :]
        for r in range(0, rows, CH):
            pos = lax.broadcasted_iota(jnp.int32, (CH, LANES), 0) + (r + offset)
            scale = jnp.where(pos >= 3 * TILE, inv[3], inv[2])
            scale = jnp.where(pos >= 2 * TILE, scale, inv[1])
            scale = jnp.where(pos >= TILE, scale, inv[0])
            du = du_ref[s, cg, r : r + CH, :]
            pay_out[0, r : r + CH, lanes] = (du * scale).astype(jnp.bfloat16)
        return 0

    lax.fori_loop(0, groups, group, 0)


def shards(streams, filters, out_weight, grad_out, counts, starts):
    _, rows, channels = streams.shape
    taps = filters.shape[1]
    width = grad_out.shape[1]
    g = channels // LANES
    vmem = pl.BlockSpec(memory_space=pltpu.VMEM)
    smem = pl.BlockSpec(memory_space=pltpu.SMEM)
    hbm = pl.BlockSpec(memory_space=pltpu.HBM)
    f32, bf16 = jnp.float32, jnp.bfloat16
    V = pltpu.VMEM
    du, inv, scale, fgrad = pl.pallas_call(
        kernel,
        out_shape=(
            V((3, g, rows + 8, LANES), f32),
            V((SLOTS, 3 * g, LANES), f32),
            V((SLOTS, 3 * g, LANES), f32),
            V((NG, 3, 8, LANES), f32),
        ),
        in_specs=[hbm, hbm, hbm, hbm, smem, smem],
        out_specs=(vmem, vmem, vmem, vmem),
        scratch_shapes=[
            V((3, rows, channels), bf16),
            V((3, taps, channels), f32),
            V((3, g, rows + 16, LANES), f32),
            V((3, g, STEP, 8, LANES), f32),
            V((NZ, NX, NC, 64, channels), bf16),
            V((rows, NY * width), bf16),
            V((2, 2, rows + 8, LANES), f32),
            V((3, g, rows + 16, LANES), f32),
            V((3, g, 8, LANES), f32),
            V((3, g, 8, LANES), f32),
            V((3, g, 8, LANES), f32),
            V((3, g, 8, LANES), f32),
            V((3, g, rows + 16, LANES), f32),
            V((SLOTS, 3 * g, LANES), f32),
            V((3 * g, LANES), f32),
            V((3 * g, LANES), f32),
            V((3 * g, LANES), f32),
            V((g, 3, 8, LANES), f32),
            V((NG, 3, 8, LANES), f32),
            V((NZ, 3, 8, LANES), f32),
            pltpu.SemaphoreType.DMA((96,)),
            pltpu.SemaphoreType.DMA((96,)),
            pltpu.SemaphoreType.DMA((4,)),
        ],
        compiler_params=pltpu.CompilerParams(
            collective_id=0, has_side_effects=True, vmem_limit_bytes=VLIM * 1024 * 1024
        ),
        cost_estimate=pl.CostEstimate(
            flops=2 * rows * channels * NY * width, bytes_accessed=12 * rows * channels, transcendentals=0
        ),
    )(streams, filters, out_weight.T, grad_out, counts, starts)
    return pl.pallas_call(
        finish,
        grid=(3,),
        out_shape=(
            jax.ShapeDtypeStruct((3, rows, channels), bf16),
            jax.ShapeDtypeStruct((3, SLOTS, channels), f32),
            jax.ShapeDtypeStruct((3, taps, channels), f32),
        ),
        in_specs=[smem, vmem, vmem, vmem, vmem],
        out_specs=(
            pl.BlockSpec((1, rows, channels), lambda s: (s, 0, 0)),
            pl.BlockSpec((1, SLOTS, channels), lambda s: (s, 0, 0)),
            pl.BlockSpec((1, taps, channels), lambda s: (s, 0, 0)),
        ),
        compiler_params=pltpu.CompilerParams(vmem_limit_bytes=20 * 1024 * 1024),
    )(starts, du, inv, scale, fgrad)


def solution(mesh):
    return jax.shard_map(
        shards,
        mesh=mesh,
        in_specs=(
            P(None, "ctx", "tp"),
            P(None, None, "tp"),
            P("tp", "ctx"),
            P("ctx", "tp"),
            P("ctx"),
            P("ctx"),
        ),
        out_specs=(P(None, "ctx", "tp"), P(None, "ctx", "tp"), P(None, None, "tp")),
        check_vma=False,
    )
```

```python
import functools

import jax
import jax.numpy as jnp
from jax import lax
from jax.experimental import pallas as pl
from jax.experimental.pallas import tpu as pltpu
from jax.sharding import PartitionSpec as P

MESH = pl.DeviceIdType.MESH
TILE = 128
LANES = 128
NZ, NX, NC, NY = 8, 4, 2, 8
NG = NX * NC
CH = 64
SLOTS = 4
STEP = 49
VLIM = 54


ORDER = (
    "b1", "f", "g01", "a0", "f", "b2", "x0", "f", "x1", "g11", "A01", "x2", "f", "A11", "g02",
    "b3", "A02", "g12", "x3", "A12", "b4", "g03", "A03", "x4", "A13", "g13", "X", "A04", "A14",
)


def kernel(
    streams_ref, filters_ref, weight_ref, grad_ref, counts_ref, starts_ref,
    du32, inv_ref, scales_ref, fgrad_ref,
    sv, fv, u32, prod, wt, gg, dyb, dc32, tail, halo, head, heads_in, zbuf,
    msc, tmx, max_prev, max_next, fsc, p1, p2,
    send, recv, hsend, hrecv, tsend, trecv, local,
):
    rows = grad_ref.shape[0]
    width = grad_ref.shape[1]
    taps = filters_ref.shape[1]
    groups = weight_ref.shape[1] // LANES
    i = lax.axis_index("ctx")
    y = lax.axis_index("tp")
    z = i // NG
    q = i % NG
    x = q // NC
    core = q % NC
    n_ctx = NZ * NG

    count = counts_ref[0]
    first = starts_ref[0]
    offset = first % TILE
    last_slot = jnp.clip((offset + count - 1) // TILE, 0, SLOTS - 1)

    def at(zz, xx, cc):
        return ((zz + NZ) % NZ) * NG + ((xx + NX) % NX) * NC + cc

    copies = []

    def push(src, dst, ctx, tp):
        k = len(copies)
        c = pltpu.make_async_remote_copy(
            src_ref=src, dst_ref=dst, send_sem=send.at[k], recv_sem=recv.at[k],
            device_id=(ctx, tp), device_id_type=MESH,
        )
        c.start()
        copies.append(c)
        return c

    up, down = (i + 1) % n_ctx, (i + n_ctx - 1) % n_ctx
    yr, yl = (y + 1) % NY, (y + NY - 1) % NY
    zr, zl = at(z + 1, x, core), at(z - 1, x, core)
    xr, xl = at(z, x + 1, core), at(z, x - 1, core)
    mate = at(z, x, 1 - core)

    get_streams = pltpu.make_async_copy(streams_ref, sv, local.at[0])
    get_streams.start()
    own_cols = pl.ds(pl.multiple_of(y * width, width), width)
    get_grad = pltpu.make_async_copy(grad_ref, gg.at[:, own_cols], local.at[1])
    get_grad.start()

    get_weight = pltpu.make_async_copy(weight_ref, wt.at[z, x, core], local.at[2])
    get_weight.start()
    get_filters = pltpu.make_async_copy(filters_ref, fv, local.at[3])
    get_filters.start()

    barrier = pltpu.get_barrier_semaphore()
    peers = [(i, yr), (i, yl), (up, y), (down, y)]
    peers += [(z * NG + (q + d) % NG, y) for d in range(1, NG)]
    peers += [(((z + d) % NZ) * NG + q, y) for d in range(1, NZ)]
    for peer in peers:
        pl.semaphore_signal(barrier, inc=1, device_id=peer, device_id_type=MESH)
    pl.semaphore_wait(barrier, len(peers))

    half = rows // 2

    def gblock(c, t):
        t = (t + NY) % NY
        return gg.at[pl.ds(c * half, half), pl.ds(pl.multiple_of(t * width, width), width)]

    def gstep(c, d):
        out = []
        own = grad_ref.at[pl.ds(c * half, half)]
        if d < 4 or c == 0:
            block = gblock(c, y - d + 1)
            out.append(push(own if d == 1 else block, block, i, yr))
        if d < 4 or c == 1:
            block = gblock(c, y + d - 1)
            out.append(push(own if d == 1 else block, block, i, yl))
        return out

    def arrived(cs):
        for c in cs:
            c.wait_recv()

    def ablock(c, zz, many=2):
        return wt.at[(zz + NZ) % NZ, pl.ds(2 * c, many), core, pl.ds(0, 32), :]

    def bpiece(zz, xx, lo=32, many=32):
        return wt.at[(zz + NZ) % NZ, (xx + NX) % NX, core, pl.ds(lo, many), :]

    def bcolumn(xx):
        return wt.at[:, (xx + NX) % NX, core, pl.ds(32, 32), :]

    def same(block, dest):
        return push(block, block, dest, y)

    def astep(c, d):
        out = []
        if d < 4 or c == 0:
            out.append(same(ablock(c, z - d + 1), zr))
        if d < 4 or c == 1:
            out.append(same(ablock(c, z + d - 1), zl))
        return out

    def bstep(d):
        many = 32 if d < 4 else 16
        return [same(bpiece(z - d + 1, x, 32, many), zr), same(bpiece(z + d - 1, x, 64 - many, many), zl)]

    def xstep(p):
        out = []
        for zz in [z + p] if p in (0, 4) else [z + p, z - p]:
            out += [same(bpiece(zz, x), xr), same(bpiece(zz, x), xl)]
        return out

    flight = {"X": []}
    mates = []
    flight["g01"] = gstep(0, 1)
    get_weight.wait()
    flight["b1"] = bstep(1)
    own = wt.at[z, x, core, pl.ds(0, 32), :]
    flight["a0"] = [same(own, at(z, x + d, core)) for d in range(1, NX)]
    flight["x0"] = xstep(0)
    flight["g11"] = gstep(1, 1)

    get_streams.wait()

    def widen(cg, _):
        lanes = pl.ds(pl.multiple_of(cg * LANES, LANES), LANES)
        for s in range(3):
            u32[s, cg, 8 : 8 + rows, :] = sv[s, :, lanes].astype(jnp.float32)
            u32[s, cg, 8 + rows :, :] = jnp.zeros((8, LANES), jnp.float32)
            tail[s, cg] = u32[s, cg, pl.ds(jnp.clip(count, 8, rows), 8), :]
        return 0

    lax.fori_loop(0, groups, widen, 0)
    tails = push(tail, halo, up, y)

    def strided(start):
        return pl.ds(start, 8, stride=STEP)

    def tapped(f, w):
        acc = f[0] * w[0]
        for j in range(1, taps):
            acc = acc + f[j] * w[j]
        return acc

    sub = lax.broadcasted_iota(jnp.int32, (8, LANES), 0) * STEP

    def forward(cg, _):
        lanes = pl.ds(pl.multiple_of(cg * LANES, LANES), LANES)
        coef = []
        for s in range(3):
            u32[s, cg, 0:8, :] = jnp.where(i > 0, halo[s, cg], 0.0)
            dc32[s, cg, rows:, :] = jnp.zeros((16, LANES), jnp.float32)
            zbuf[s, cg] = jnp.zeros((rows + 16, LANES), jnp.float32)
            for k in range(taps, 8):
                fsc[cg, s, k : k + 1, :] = jnp.zeros((1, LANES), jnp.float32)
            coef.append([fv[s, pl.ds(j, 1), lanes] for j in range(taps)])

        spread = [[jnp.broadcast_to(f, (8, LANES)) for f in fs] for fs in coef]
        window = [[u32[s, cg, strided(8 - j), :] for j in range(1, taps)] for s in range(3)]
        for k in range(STEP):
            c = []
            for s in range(3):
                window[s] = [u32[s, cg, strided(8 + k), :]] + window[s][: taps - 1]
                c.append(tapped(spread[s], window[s]))
            prod[0, cg, k] = c[1] * c[2]
            prod[1, cg, k] = c[0] * c[2]
            prod[2, cg, k] = c[0] * c[1]
        return 0

    def project(b, slot):
        cols = pl.ds(pl.multiple_of(b * 256, 256), 256)
        w = wt[:, :, :, :, cols].reshape(NZ * NG * 64, 256)
        dy = jnp.dot(gg[...], w, preferred_element_type=jnp.float32)
        dy = dy.astype(jnp.bfloat16).astype(jnp.float32)
        dyb[slot, 0, :rows, :] = dy[:, :LANES]
        dyb[slot, 1, :rows, :] = dy[:, LANES:]

    def gate(b, slot):
        for e in range(2):
            cg = 2 * b + e
            for s in range(3):
                acc = [jnp.zeros((8, LANES), jnp.float32)] * taps
                window = [u32[s, cg, strided(8 - j), :] for j in range(1, taps)]
                for k in range(STEP):
                    window = [u32[s, cg, strided(8 + k), :]] + window[: taps - 1]
                    dc = jnp.where(sub < count - k, dyb[slot, e, strided(k), :] * prod[s, cg, k], 0.0)
                    dc = dc.astype(jnp.bfloat16).astype(jnp.float32)
                    dc32[s, cg, strided(k), :] = dc
                    acc = [acc[j] + dc * window[j] for j in range(taps)]
                for j in range(taps):
                    fsc[cg, s, j : j + 1, :] = acc[j].sum(0, keepdims=True)
                head[s, cg] = dc32[s, cg, 0:8, :]

    done = 0
    for token in ORDER:
        kind = token[0]
        if kind == "f":
            if done == 0:
                get_filters.wait()
                tails.wait_recv()
            lax.fori_loop(done, done + groups // 4, forward, 0)
            done += groups // 4
            continue
        arrived(flight[token])
        if kind == "g" or kind == "A":
            c, d = int(token[1]), int(token[2])
            if d < 4:
                flight[f"{kind}{c}{d + 1}"] = (gstep if kind == "g" else astep)(c, d + 1)
            if kind == "A" and c == 1:
                mates.append(same(ablock(0, z - d, NX), mate))
                if d < 4:
                    mates.append(same(ablock(0, z + d, NX), mate))
        elif kind == "a":
            flight["A01"], flight["A11"] = astep(0, 1), astep(1, 1)
            mates.append(same(ablock(0, z, NX), mate))
        elif kind == "b":
            d = int(token[1])
            if d < 4:
                flight[f"b{d + 1}"] = bstep(d + 1)
            else:
                mates.append(same(bcolumn(x), mate))
            flight[f"x{d}"] = xstep(d)
        elif kind == "x":
            p = int(token[1])
            if p < 4:
                flight["X"].append(same(bpiece(z + p, x - 1), xr))
            if p > 0:
                flight["X"].append(same(bpiece(z - p, x + 1), xl))
            if p == 4:
                mates += [same(bcolumn(x - 1), mate), same(bcolumn(x + 1), mate)]
        else:
            mates.append(same(bcolumn(x + 2), mate))
            sent = len(copies) - 3
            for c in copies[:sent]:
                c.wait_send()
    get_grad.wait()
    arrived(mates)
    arrived(flight["g04"])
    arrived(flight["g14"])

    blocks = groups // 2

    def head_copy(b):
        two = pl.ds(2 * b, 2)
        return pltpu.make_async_remote_copy(
            src_ref=head.at[:, two], dst_ref=heads_in.at[:, two], send_sem=hsend.at[b], recv_sem=hrecv.at[b],
            device_id=(down, y), device_id_type=MESH,
        )

    def term_copy(to, me):
        return pltpu.make_async_remote_copy(
            src_ref=fsc.at[to], dst_ref=p1.at[me], send_sem=tsend.at[to], recv_sem=trecv.at[me],
            device_id=(z * NG + to, y), device_id_type=MESH,
        )

    def leave(b):
        head_copy(b).start()
        for e in range(2):
            @pl.when(2 * b + e != q)
            def _():
                term_copy(2 * b + e, q).start()

    def both(b, _):
        gate(b - 1, (b + 1) % 2)
        project(b, b % 2)
        leave(b - 1)
        return 0

    project(0, 0)
    lax.fori_loop(1, blocks, both, 0)
    gate(blocks - 1, (blocks - 1) % 2)
    leave(blocks - 1)

    held = jnp.clip(count, half, rows)

    def backward(b, _):
        head_copy(b).wait_recv()
        lax.fori_loop(2 * b, 2 * b + 2, group_back, 0)
        return 0

    def group_back(cg, _):
        lanes = pl.ds(pl.multiple_of(cg * LANES, LANES), LANES)
        for s in range(3):
            zbuf[s, cg, half : half + 8, :] = jnp.where(i < n_ctx - 1, heads_in[s, cg], 0.0)

        leap = (rows - half + 8) // 8
        for m in range(leap):
            to = pl.ds(half + m, 8, stride=leap)
            for s in range(3):
                dc32[s, cg, to, :] += zbuf[s, cg, pl.ds(rows + m - held, 8, stride=leap), :]

        low = (sub + offset) // TILE
        border = (low + 1) * TILE - offset - sub
        for s in range(3):
            f = [jnp.broadcast_to(fv[s, pl.ds(j, 1), lanes], (8, LANES)) for j in range(taps)]
            window = [dc32[s, cg, strided(j), :] for j in range(taps - 1)]
            before = jnp.zeros((8, LANES), jnp.float32)
            after = before
            for k in range(STEP):
                window = window[-(taps - 1) :] + [dc32[s, cg, strided(k + taps - 1), :]]
                du = jnp.where(sub < count - k, tapped(f, window), 0.0)
                du32[s, cg, strided(k), :] = du
                size = jnp.abs(du)
                before = jnp.maximum(before, jnp.where(border > k, size, 0.0))
                after = jnp.maximum(after, jnp.where(border > k, 0.0, size))
            for k in range(SLOTS):
                top = jnp.maximum(jnp.where(low == k, before, 0.0), jnp.where(low == k - 1, after, 0.0))
                msc[k, pl.ds(s * groups + cg, 1), :] = top.max(0, keepdims=True)
        return 0

    lax.fori_loop(0, blocks // 2, backward, 0)
    part = fsc[q]
    for d in range(1, NG):
        source = (q + d) % NG
        term_copy(source, source).wait_recv()
        part = part + p1[source]
    p2[z] = part
    f2 = []
    for d in range(1, NZ):
        f2.append(push(p2.at[z], p2.at[z], ((z + d) % NZ) * NG + q, y))
    lax.fori_loop(blocks // 2, blocks, backward, 0)
    tmx[...] = msc[last_slot]
    to_next = push(tmx, max_prev, up, y)
    to_prev = push(msc.at[0], max_next, down, y)

    arrived(f2)
    total = p2[0]
    for d in range(1, NZ):
        total = total + p2[d]
    fgrad_ref[q] = total
    f3 = []
    for d in range(1, NG):
        f3.append(push(fgrad_ref.at[q], fgrad_ref.at[q], z * NG + (q + d) % NG, y))

    to_next.wait_recv()
    to_prev.wait_recv()
    prev = jnp.where(offset != 0, max_prev[...], 0.0)
    follow = jnp.where((first + count) % TILE != 0, max_next[...], 0.0)
    for k in range(SLOTS):
        top = msc[k]
        if k == 0:
            top = jnp.maximum(top, prev)
        top = jnp.maximum(top, jnp.where(last_slot == k, follow, 0.0))
        scale = top + 1e-6
        inv_ref[k] = 1.0 / scale
        scales_ref[k] = jnp.where(last_slot >= k, scale, 0.0)

    arrived(f3)
    for c in copies[sent:]:
        c.wait_send()
    for b in range(blocks):
        head_copy(b).wait_send()
    for d in range(1, NG):
        term_copy((q + d) % NG, q).wait_send()


def finish(starts_ref, du_ref, inv_ref, scale_ref, fgrad_ref, pay_out, scales_out, fgrad_out):
    s = pl.program_id(0)
    groups, rows = du_ref.shape[1], pay_out.shape[1]
    offset = starts_ref[0] % TILE
    taps = fgrad_out.shape[1]

    def group(cg, _):
        lanes = pl.ds(pl.multiple_of(cg * LANES, LANES), LANES)
        row = pl.ds(s * groups + cg, 1)
        inv = [inv_ref[k, row, :] for k in range(SLOTS)]
        for k in range(SLOTS):
            scales_out[0, k : k + 1, lanes] = scale_ref[k, row, :]
        fgrad_out[0, :, lanes] = fgrad_ref[cg, s, :taps, :]
        for r in range(0, rows, CH):
            pos = lax.broadcasted_iota(jnp.int32, (CH, LANES), 0) + (r + offset)
            scale = jnp.where(pos >= 3 * TILE, inv[3], inv[2])
            scale = jnp.where(pos >= 2 * TILE, scale, inv[1])
            scale = jnp.where(pos >= TILE, scale, inv[0])
            du = du_ref[s, cg, r : r + CH, :]
            pay_out[0, r : r + CH, lanes] = (du * scale).astype(jnp.bfloat16)
        return 0

    lax.fori_loop(0, groups, group, 0)


def shards(streams, filters, out_weight, grad_out, counts, starts):
    _, rows, channels = streams.shape
    taps = filters.shape[1]
    width = grad_out.shape[1]
    g = channels // LANES
    vmem = pl.BlockSpec(memory_space=pltpu.VMEM)
    smem = pl.BlockSpec(memory_space=pltpu.SMEM)
    hbm = pl.BlockSpec(memory_space=pltpu.HBM)
    f32, bf16 = jnp.float32, jnp.bfloat16
    V = pltpu.VMEM
    du, inv, scale, fgrad = pl.pallas_call(
        kernel,
        out_shape=(
            V((3, g, rows + 8, LANES), f32),
            V((SLOTS, 3 * g, LANES), f32),
            V((SLOTS, 3 * g, LANES), f32),
            V((NG, 3, 8, LANES), f32),
        ),
        in_specs=[hbm, hbm, hbm, hbm, smem, smem],
        out_specs=(vmem, vmem, vmem, vmem),
        scratch_shapes=[
            V((3, rows, channels), bf16),
            V((3, taps, channels), f32),
            V((3, g, rows + 16, LANES), f32),
            V((3, g, STEP, 8, LANES), f32),
            V((NZ, NX, NC, 64, channels), bf16),
            V((rows, NY * width), bf16),
            V((2, 2, rows + 8, LANES), f32),
            V((3, g, rows + 16, LANES), f32),
            V((3, g, 8, LANES), f32),
            V((3, g, 8, LANES), f32),
            V((3, g, 8, LANES), f32),
            V((3, g, 8, LANES), f32),
            V((3, g, rows + 16, LANES), f32),
            V((SLOTS, 3 * g, LANES), f32),
            V((3 * g, LANES), f32),
            V((3 * g, LANES), f32),
            V((3 * g, LANES), f32),
            V((g, 3, 8, LANES), f32),
            V((NG, 3, 8, LANES), f32),
            V((NZ, 3, 8, LANES), f32),
            pltpu.SemaphoreType.DMA((112,)),
            pltpu.SemaphoreType.DMA((112,)),
            pltpu.SemaphoreType.DMA((g // 2,)),
            pltpu.SemaphoreType.DMA((g // 2,)),
            pltpu.SemaphoreType.DMA((NG,)),
            pltpu.SemaphoreType.DMA((NG,)),
            pltpu.SemaphoreType.DMA((4,)),
        ],
        compiler_params=pltpu.CompilerParams(
            collective_id=0, has_side_effects=True, vmem_limit_bytes=VLIM * 1024 * 1024
        ),
        cost_estimate=pl.CostEstimate(
            flops=2 * rows * channels * NY * width, bytes_accessed=12 * rows * channels, transcendentals=0
        ),
    )(streams, filters, out_weight.T, grad_out, counts, starts)
    return pl.pallas_call(
        finish,
        grid=(3,),
        out_shape=(
            jax.ShapeDtypeStruct((3, rows, channels), bf16),
            jax.ShapeDtypeStruct((3, SLOTS, channels), f32),
            jax.ShapeDtypeStruct((3, taps, channels), f32),
        ),
        in_specs=[smem, vmem, vmem, vmem, vmem],
        out_specs=(
            pl.BlockSpec((1, rows, channels), lambda s: (s, 0, 0)),
            pl.BlockSpec((1, SLOTS, channels), lambda s: (s, 0, 0)),
            pl.BlockSpec((1, taps, channels), lambda s: (s, 0, 0)),
        ),
        compiler_params=pltpu.CompilerParams(vmem_limit_bytes=20 * 1024 * 1024),
    )(starts, du, inv, scale, fgrad)


def solution(mesh):
    return jax.shard_map(
        shards,
        mesh=mesh,
        in_specs=(
            P(None, "ctx", "tp"),
            P(None, None, "tp"),
            P("tp", "ctx"),
            P("ctx", "tp"),
            P("ctx"),
            P("ctx"),
        ),
        out_specs=(P(None, "ctx", "tp"), P(None, "ctx", "tp"), P(None, None, "tp")),
        check_vma=False,
    )
```

```python
import functools

import jax
import jax.numpy as jnp
from jax import lax
from jax.experimental import pallas as pl
from jax.experimental.pallas import tpu as pltpu
from jax.sharding import PartitionSpec as P

MESH = pl.DeviceIdType.MESH
TILE = 128
LANES = 128
NZ, NX, NC, NY = 8, 4, 2, 8
NG = NX * NC
CH = 64
SLOTS = 4
WIDE = 512
PER = WIDE // LANES
STEP = 49
VLIM = 54


ORDER = (
    "b1", "f", "g01", "a0", "f", "b2", "x0", "f", "x1", "g11", "A01", "x2", "f", "A11", "g02",
    "b3", "A02", "g12", "x3", "A12", "b4", "g03", "A03", "x4", "A13", "g13", "X", "A04", "A14",
)


def kernel(
    streams_ref, filters_ref, weight_ref, grad_ref, counts_ref, starts_ref,
    du32, inv_ref, scales_ref, fgrad_ref,
    sv, fv, u32, prod, wt, gg, dyb, dc32, tail, halo, head, heads_in, zbuf,
    msc, tmx, max_prev, max_next, fsc, p1, p2,
    send, recv, hsend, hrecv, tsend, trecv, local,
):
    rows = grad_ref.shape[0]
    width = grad_ref.shape[1]
    taps = filters_ref.shape[1]
    groups = weight_ref.shape[1] // LANES
    i = lax.axis_index("ctx")
    y = lax.axis_index("tp")
    z = i // NG
    q = i % NG
    x = q // NC
    core = q % NC
    n_ctx = NZ * NG

    count = counts_ref[0]
    first = starts_ref[0]
    offset = first % TILE
    last_slot = jnp.clip((offset + count - 1) // TILE, 0, SLOTS - 1)

    def at(zz, xx, cc):
        return ((zz + NZ) % NZ) * NG + ((xx + NX) % NX) * NC + cc

    copies = []

    def push(src, dst, ctx, tp):
        k = len(copies)
        c = pltpu.make_async_remote_copy(
            src_ref=src, dst_ref=dst, send_sem=send.at[k], recv_sem=recv.at[k],
            device_id=(ctx, tp), device_id_type=MESH,
        )
        c.start()
        copies.append(c)
        return c

    up, down = (i + 1) % n_ctx, (i + n_ctx - 1) % n_ctx
    yr, yl = (y + 1) % NY, (y + NY - 1) % NY
    zr, zl = at(z + 1, x, core), at(z - 1, x, core)
    xr, xl = at(z, x + 1, core), at(z, x - 1, core)
    mate = at(z, x, 1 - core)

    get_streams = pltpu.make_async_copy(streams_ref, sv, local.at[0])
    get_streams.start()
    own_cols = pl.ds(pl.multiple_of(y * width, width), width)
    get_grad = pltpu.make_async_copy(grad_ref, gg.at[:, own_cols], local.at[1])
    get_grad.start()

    get_weight = pltpu.make_async_copy(weight_ref, wt.at[z, x, core], local.at[2])
    get_weight.start()
    get_filters = pltpu.make_async_copy(filters_ref, fv, local.at[3])
    get_filters.start()

    barrier = pltpu.get_barrier_semaphore()
    peers = [(i, yr), (i, yl), (up, y), (down, y)]
    peers += [(z * NG + (q + d) % NG, y) for d in range(1, NG)]
    peers += [(((z + d) % NZ) * NG + q, y) for d in range(1, NZ)]
    for peer in peers:
        pl.semaphore_signal(barrier, inc=1, device_id=peer, device_id_type=MESH)
    pl.semaphore_wait(barrier, len(peers))

    half = rows // 2

    def gblock(c, t):
        t = (t + NY) % NY
        return gg.at[pl.ds(c * half, half), pl.ds(pl.multiple_of(t * width, width), width)]

    def gstep(c, d):
        out = []
        own = grad_ref.at[pl.ds(c * half, half)]
        if d < 4 or c == 0:
            block = gblock(c, y - d + 1)
            out.append(push(own if d == 1 else block, block, i, yr))
        if d < 4 or c == 1:
            block = gblock(c, y + d - 1)
            out.append(push(own if d == 1 else block, block, i, yl))
        return out

    def arrived(cs):
        for c in cs:
            c.wait_recv()

    def ablock(c, zz, many=2):
        return wt.at[(zz + NZ) % NZ, pl.ds(2 * c, many), core, pl.ds(0, 32), :]

    def bpiece(zz, xx, lo=32, many=32):
        return wt.at[(zz + NZ) % NZ, (xx + NX) % NX, core, pl.ds(lo, many), :]

    def bcolumn(xx):
        return wt.at[:, (xx + NX) % NX, core, pl.ds(32, 32), :]

    def same(block, dest):
        return push(block, block, dest, y)

    def astep(c, d):
        out = []
        if d < 4 or c == 0:
            out.append(same(ablock(c, z - d + 1), zr))
        if d < 4 or c == 1:
            out.append(same(ablock(c, z + d - 1), zl))
        return out

    def bstep(d):
        many = 32 if d < 4 else 16
        return [same(bpiece(z - d + 1, x, 32, many), zr), same(bpiece(z + d - 1, x, 64 - many, many), zl)]

    def xstep(p):
        out = []
        for zz in [z + p] if p in (0, 4) else [z + p, z - p]:
            out += [same(bpiece(zz, x), xr), same(bpiece(zz, x), xl)]
        return out

    flight = {"X": []}
    mates = []
    flight["g01"] = gstep(0, 1)
    get_weight.wait()
    flight["b1"] = bstep(1)
    own = wt.at[z, x, core, pl.ds(0, 32), :]
    flight["a0"] = [same(own, at(z, x + d, core)) for d in range(1, NX)]
    flight["x0"] = xstep(0)
    flight["g11"] = gstep(1, 1)

    get_streams.wait()

    def widen(cg, _):
        lanes = pl.ds(pl.multiple_of(cg * LANES, LANES), LANES)
        for s in range(3):
            u32[s, cg, 8 : 8 + rows, :] = sv[s, :, lanes].astype(jnp.float32)
            u32[s, cg, 8 + rows :, :] = jnp.zeros((8, LANES), jnp.float32)
            tail[s, cg] = u32[s, cg, pl.ds(jnp.clip(count, 8, rows), 8), :]
        return 0

    lax.fori_loop(0, groups, widen, 0)
    tails = push(tail, halo, up, y)

    def strided(start):
        return pl.ds(start, 8, stride=STEP)

    def tapped(f, w):
        acc = f[0] * w[0]
        for j in range(1, taps):
            acc = acc + f[j] * w[j]
        return acc

    sub = lax.broadcasted_iota(jnp.int32, (8, LANES), 0) * STEP

    def forward(cg, _):
        lanes = pl.ds(pl.multiple_of(cg * LANES, LANES), LANES)
        coef = []
        for s in range(3):
            u32[s, cg, 0:8, :] = jnp.where(i > 0, halo[s, cg], 0.0)
            dc32[s, cg, rows:, :] = jnp.zeros((16, LANES), jnp.float32)
            zbuf[s, cg] = jnp.zeros((rows + 16, LANES), jnp.float32)
            for k in range(taps, 8):
                fsc[cg, s, k : k + 1, :] = jnp.zeros((1, LANES), jnp.float32)
            coef.append([fv[s, pl.ds(j, 1), lanes] for j in range(taps)])

        spread = [[jnp.broadcast_to(f, (8, LANES)) for f in fs] for fs in coef]
        window = [[u32[s, cg, strided(8 - j), :] for j in range(1, taps)] for s in range(3)]
        for k in range(STEP):
            c = []
            for s in range(3):
                window[s] = [u32[s, cg, strided(8 + k), :]] + window[s][: taps - 1]
                c.append(tapped(spread[s], window[s]))
            prod[0, cg, k] = c[1] * c[2]
            prod[1, cg, k] = c[0] * c[2]
            prod[2, cg, k] = c[0] * c[1]
        return 0

    def project(b, slot):
        cols = pl.ds(pl.multiple_of(b * WIDE, WIDE), WIDE)
        w = wt[:, :, :, :, cols].reshape(NZ * NG * 64, WIDE)
        dy = jnp.dot(gg[...], w, preferred_element_type=jnp.float32)
        dy = dy.astype(jnp.bfloat16).astype(jnp.float32)
        for e in range(PER):
            dyb[slot, e, :rows, :] = dy[:, e * LANES : (e + 1) * LANES]

    def gate(b, slot):
        for e in range(PER):
            cg = PER * b + e
            for s in range(3):
                acc = [jnp.zeros((8, LANES), jnp.float32)] * taps
                window = [u32[s, cg, strided(8 - j), :] for j in range(1, taps)]
                for k in range(STEP):
                    window = [u32[s, cg, strided(8 + k), :]] + window[: taps - 1]
                    dc = jnp.where(sub < count - k, dyb[slot, e, strided(k), :] * prod[s, cg, k], 0.0)
                    dc = dc.astype(jnp.bfloat16).astype(jnp.float32)
                    dc32[s, cg, strided(k), :] = dc
                    acc = [acc[j] + dc * window[j] for j in range(taps)]
                for j in range(taps):
                    fsc[cg, s, j : j + 1, :] = acc[j].sum(0, keepdims=True)
                head[s, cg] = dc32[s, cg, 0:8, :]

    done = 0
    for token in ORDER:
        kind = token[0]
        if kind == "f":
            if done == 0:
                get_filters.wait()
                tails.wait_recv()
            lax.fori_loop(done, done + groups // 4, forward, 0)
            done += groups // 4
            continue
        arrived(flight[token])
        if kind == "g" or kind == "A":
            c, d = int(token[1]), int(token[2])
            if d < 4:
                flight[f"{kind}{c}{d + 1}"] = (gstep if kind == "g" else astep)(c, d + 1)
            if kind == "A" and c == 1:
                mates.append(same(ablock(0, z - d, NX), mate))
                if d < 4:
                    mates.append(same(ablock(0, z + d, NX), mate))
        elif kind == "a":
            flight["A01"], flight["A11"] = astep(0, 1), astep(1, 1)
            mates.append(same(ablock(0, z, NX), mate))
        elif kind == "b":
            d = int(token[1])
            if d < 4:
                flight[f"b{d + 1}"] = bstep(d + 1)
            else:
                mates.append(same(bcolumn(x), mate))
            flight[f"x{d}"] = xstep(d)
        elif kind == "x":
            p = int(token[1])
            if p < 4:
                flight["X"].append(same(bpiece(z + p, x - 1), xr))
            if p > 0:
                flight["X"].append(same(bpiece(z - p, x + 1), xl))
            if p == 4:
                mates += [same(bcolumn(x - 1), mate), same(bcolumn(x + 1), mate)]
        else:
            mates.append(same(bcolumn(x + 2), mate))
            sent = len(copies) - 3
            for c in copies[:sent]:
                c.wait_send()
    get_grad.wait()
    arrived(mates)
    arrived(flight["g04"])
    arrived(flight["g14"])

    blocks = groups // PER

    def head_copy(b):
        some = pl.ds(PER * b, PER)
        return pltpu.make_async_remote_copy(
            src_ref=head.at[:, some], dst_ref=heads_in.at[:, some], send_sem=hsend.at[b], recv_sem=hrecv.at[b],
            device_id=(down, y), device_id_type=MESH,
        )

    def term_copy(to, me):
        return pltpu.make_async_remote_copy(
            src_ref=fsc.at[to], dst_ref=p1.at[me], send_sem=tsend.at[to], recv_sem=trecv.at[me],
            device_id=(z * NG + to, y), device_id_type=MESH,
        )

    def leave(b):
        head_copy(b).start()
        for e in range(PER):
            @pl.when(PER * b + e != q)
            def _():
                term_copy(PER * b + e, q).start()

    def both(b, _):
        gate(b - 1, (b + 1) % 2)
        project(b, b % 2)
        leave(b - 1)
        return 0

    project(0, 0)
    lax.fori_loop(1, blocks, both, 0)
    gate(blocks - 1, (blocks - 1) % 2)
    leave(blocks - 1)

    held = jnp.clip(count, half, rows)

    def backward(b, _):
        head_copy(b).wait_recv()
        lax.fori_loop(PER * b, PER * b + PER, group_back, 0)
        return 0

    def group_back(cg, _):
        lanes = pl.ds(pl.multiple_of(cg * LANES, LANES), LANES)
        for s in range(3):
            zbuf[s, cg, half : half + 8, :] = jnp.where(i < n_ctx - 1, heads_in[s, cg], 0.0)

        leap = (rows - half + 8) // 8
        for m in range(leap):
            to = pl.ds(half + m, 8, stride=leap)
            for s in range(3):
                dc32[s, cg, to, :] += zbuf[s, cg, pl.ds(rows + m - held, 8, stride=leap), :]

        low = (sub + offset) // TILE
        border = (low + 1) * TILE - offset - sub
        for s in range(3):
            f = [jnp.broadcast_to(fv[s, pl.ds(j, 1), lanes], (8, LANES)) for j in range(taps)]
            window = [dc32[s, cg, strided(j), :] for j in range(taps - 1)]
            before = jnp.zeros((8, LANES), jnp.float32)
            after = before
            for k in range(STEP):
                window = window[-(taps - 1) :] + [dc32[s, cg, strided(k + taps - 1), :]]
                du = jnp.where(sub < count - k, tapped(f, window), 0.0)
                du32[s, cg, strided(k), :] = du
                size = jnp.abs(du)
                before = jnp.maximum(before, jnp.where(border > k, size, 0.0))
                after = jnp.maximum(after, jnp.where(border > k, 0.0, size))
            for k in range(SLOTS):
                top = jnp.maximum(jnp.where(low == k, before, 0.0), jnp.where(low == k - 1, after, 0.0))
                msc[k, pl.ds(s * groups + cg, 1), :] = top.max(0, keepdims=True)
        return 0

    lax.fori_loop(0, blocks // 2, backward, 0)
    part = fsc[q]
    for d in range(1, NG):
        source = (q + d) % NG
        term_copy(source, source).wait_recv()
        part = part + p1[source]
    p2[z] = part
    f2 = []
    for d in range(1, NZ):
        f2.append(push(p2.at[z], p2.at[z], ((z + d) % NZ) * NG + q, y))
    lax.fori_loop(blocks // 2, blocks, backward, 0)
    tmx[...] = msc[last_slot]
    to_next = push(tmx, max_prev, up, y)
    to_prev = push(msc.at[0], max_next, down, y)

    arrived(f2)
    total = p2[0]
    for d in range(1, NZ):
        total = total + p2[d]
    fgrad_ref[q] = total
    f3 = []
    for d in range(1, NG):
        f3.append(push(fgrad_ref.at[q], fgrad_ref.at[q], z * NG + (q + d) % NG, y))

    to_next.wait_recv()
    to_prev.wait_recv()
    prev = jnp.where(offset != 0, max_prev[...], 0.0)
    follow = jnp.where((first + count) % TILE != 0, max_next[...], 0.0)
    for k in range(SLOTS):
        top = msc[k]
        if k == 0:
            top = jnp.maximum(top, prev)
        top = jnp.maximum(top, jnp.where(last_slot == k, follow, 0.0))
        scale = top + 1e-6
        inv_ref[k] = 1.0 / scale
        scales_ref[k] = jnp.where(last_slot >= k, scale, 0.0)

    arrived(f3)
    for c in copies[sent:]:
        c.wait_send()
    for b in range(blocks):
        head_copy(b).wait_send()
    for d in range(1, NG):
        term_copy((q + d) % NG, q).wait_send()


def finish(starts_ref, du_ref, inv_ref, scale_ref, fgrad_ref, pay_out, scales_out, fgrad_out):
    s = pl.program_id(0)
    groups, rows = du_ref.shape[1], pay_out.shape[1]
    offset = starts_ref[0] % TILE
    taps = fgrad_out.shape[1]

    def group(cg, _):
        lanes = pl.ds(pl.multiple_of(cg * LANES, LANES), LANES)
        row = pl.ds(s * groups + cg, 1)
        inv = [inv_ref[k, row, :] for k in range(SLOTS)]
        for k in range(SLOTS):
            scales_out[0, k : k + 1, lanes] = scale_ref[k, row, :]
        fgrad_out[0, :, lanes] = fgrad_ref[cg, s, :taps, :]
        for r in range(0, rows, CH):
            pos = lax.broadcasted_iota(jnp.int32, (CH, LANES), 0) + (r + offset)
            scale = jnp.where(pos >= 3 * TILE, inv[3], inv[2])
            scale = jnp.where(pos >= 2 * TILE, scale, inv[1])
            scale = jnp.where(pos >= TILE, scale, inv[0])
            du = du_ref[s, cg, r : r + CH, :]
            pay_out[0, r : r + CH, lanes] = (du * scale).astype(jnp.bfloat16)
        return 0

    lax.fori_loop(0, groups, group, 0)


def shards(streams, filters, out_weight, grad_out, counts, starts):
    _, rows, channels = streams.shape
    taps = filters.shape[1]
    width = grad_out.shape[1]
    g = channels // LANES
    vmem = pl.BlockSpec(memory_space=pltpu.VMEM)
    smem = pl.BlockSpec(memory_space=pltpu.SMEM)
    hbm = pl.BlockSpec(memory_space=pltpu.HBM)
    f32, bf16 = jnp.float32, jnp.bfloat16
    V = pltpu.VMEM
    du, inv, scale, fgrad = pl.pallas_call(
        kernel,
        out_shape=(
            V((3, g, rows + 8, LANES), f32),
            V((SLOTS, 3 * g, LANES), f32),
            V((SLOTS, 3 * g, LANES), f32),
            V((NG, 3, 8, LANES), f32),
        ),
        in_specs=[hbm, hbm, hbm, hbm, smem, smem],
        out_specs=(vmem, vmem, vmem, vmem),
        scratch_shapes=[
            V((3, rows, channels), bf16),
            V((3, taps, channels), f32),
            V((3, g, rows + 16, LANES), f32),
            V((3, g, STEP, 8, LANES), f32),
            V((NZ, NX, NC, 64, channels), bf16),
            V((rows, NY * width), bf16),
            V((2, PER, rows + 8, LANES), f32),
            V((3, g, rows + 16, LANES), f32),
            V((3, g, 8, LANES), f32),
            V((3, g, 8, LANES), f32),
            V((3, g, 8, LANES), f32),
            V((3, g, 8, LANES), f32),
            V((3, g, rows + 16, LANES), f32),
            V((SLOTS, 3 * g, LANES), f32),
            V((3 * g, LANES), f32),
            V((3 * g, LANES), f32),
            V((3 * g, LANES), f32),
            V((g, 3, 8, LANES), f32),
            V((NG, 3, 8, LANES), f32),
            V((NZ, 3, 8, LANES), f32),
            pltpu.SemaphoreType.DMA((112,)),
            pltpu.SemaphoreType.DMA((112,)),
            pltpu.SemaphoreType.DMA((g // 2,)),
            pltpu.SemaphoreType.DMA((g // 2,)),
            pltpu.SemaphoreType.DMA((NG,)),
            pltpu.SemaphoreType.DMA((NG,)),
            pltpu.SemaphoreType.DMA((4,)),
        ],
        compiler_params=pltpu.CompilerParams(
            collective_id=0, has_side_effects=True, vmem_limit_bytes=VLIM * 1024 * 1024
        ),
        cost_estimate=pl.CostEstimate(
            flops=2 * rows * channels * NY * width, bytes_accessed=12 * rows * channels, transcendentals=0
        ),
    )(streams, filters, out_weight.T, grad_out, counts, starts)
    return pl.pallas_call(
        finish,
        grid=(3,),
        out_shape=(
            jax.ShapeDtypeStruct((3, rows, channels), bf16),
            jax.ShapeDtypeStruct((3, SLOTS, channels), f32),
            jax.ShapeDtypeStruct((3, taps, channels), f32),
        ),
        in_specs=[smem, vmem, vmem, vmem, vmem],
        out_specs=(
            pl.BlockSpec((1, rows, channels), lambda s: (s, 0, 0)),
            pl.BlockSpec((1, SLOTS, channels), lambda s: (s, 0, 0)),
            pl.BlockSpec((1, taps, channels), lambda s: (s, 0, 0)),
        ),
        compiler_params=pltpu.CompilerParams(vmem_limit_bytes=20 * 1024 * 1024),
    )(starts, du, inv, scale, fgrad)


def solution(mesh):
    return jax.shard_map(
        shards,
        mesh=mesh,
        in_specs=(
            P(None, "ctx", "tp"),
            P(None, None, "tp"),
            P("tp", "ctx"),
            P("ctx", "tp"),
            P("ctx"),
            P("ctx"),
        ),
        out_specs=(P(None, "ctx", "tp"), P(None, "ctx", "tp"), P(None, None, "tp")),
        check_vma=False,
    )
```
